128 devices in a mesh: tm: 4 (over y_hi, core), ha: 4 (over x), wa: 8 (over y_lo, z).
Axes of the slice: x: 4, y: 4 (y_hi: 2, y_lo: 2; y = y_hi * 2 + y_lo), z: 4, core: 2. Of those that a mesh axis runs over, the one named last changes fastest.
Arguments:
- queries: bfloat16 [1, 4, 64, 128, 1536], P(None, 'tm', 'ha', 'wa'), may hold values from -6 to 6
- tile_keys: bfloat16 [1, 4, 64, 128, 1536], P(None, 'tm', 'ha', 'wa'), may hold values from -6 to 6
- values: bfloat16 [1, 4, 64, 128, 1536], P(None, 'tm', 'ha', 'wa'), may hold values from -6 to 6
- probes: bfloat16 [1, 4, 64, 128, 1536], P(None, 'tm', 'ha', 'wa'), may hold values from -6 to 6
- anchors: bfloat16 [1, 4, 64, 128, 1536], P(None, 'tm', 'ha', 'wa'), may hold values from -6 to 6
- upstream: bfloat16 [1, 4, 64, 128, 1536], P(None, 'tm', 'ha', 'wa'), may hold values from -6 to 6
Outputs:
- query_grad: bfloat16 [1, 4, 64, 128, 1536], P(None, 'tm', 'ha', 'wa')
- key_grad: bfloat16 [1, 4, 64, 128, 1536], P(None, 'tm', 'ha', 'wa')
- value_grad: bfloat16 [1, 4, 64, 128, 1536], P(None, 'tm', 'ha', 'wa')
- probe_grad: bfloat16 [1, 4, 64, 128, 1536], P(None, 'tm', 'ha', 'wa')
- anchor_grad: bfloat16 [1, 4, 64, 128, 1536], P(None, 'tm', 'ha', 'wa')
The draws below stay inside these ranges and needn't reach their ends.
All inputs are finite; a program needn't handle non-finite values.
Results may differ from the reference program's by a relative error of at most 0.025.
Values may be sent and summed in bfloat16 or wider, within the bound.
No kernel may reach another device: no remote copies, remote signals or barrier semaphores. Data moves between devices by JAX's collectives and lax.ppermute only.
A program may use at most 192 MiB of HBM per device.

```python
import jax
import jax.numpy as jnp
from jax import lax

HEADS = 12
HEAD_DIM = 128
TILE = 16
VIDEOS = 1
WIDTH = 1536
FRAMES = 4
GRID_H = 64
GRID_W = 128


def sign_pattern(key):
    flips = jax.random.bernoulli(jax.random.fold_in(key, 97), 0.5, (WIDTH,))
    return jnp.where(flips, 1.0, -1.0).astype(jnp.float32)


def full_shape():
    return (VIDEOS, FRAMES, GRID_H, GRID_W, WIDTH)


def plain_normal(key):
    return jnp.clip(jax.random.normal(key, full_shape(), jnp.float32), -6.0, 6.0).astype(jnp.bfloat16)


def draw_queries(key, part):
    key = jax.random.fold_in(key, 1)
    return plain_normal(key)


def draw_tile_keys(key, part):
    key = jax.random.fold_in(key, 2)
    return plain_normal(key)


def draw_probes(key, part):
    key = jax.random.fold_in(key, 3)
    return plain_normal(key)


def draw_anchors(key, part):
    key = jax.random.fold_in(key, 4)
    return plain_normal(key)


def block_scale(stream_key, shape, shards, low, largest):
    factor_of, own = 1.0, jax.random.fold_in(stream_key, 6)
    for axis_at, shards_of in shards:
        steps = jnp.exp(jax.random.uniform(jax.random.fold_in(own, axis_at), (shards_of,), jnp.float32, low / len(shards), largest / len(shards)))
        factor_of = factor_of * jnp.repeat(steps, shape[axis_at] // shards_of).reshape([-1 if axis == axis_at else 1 for axis in range(len(shape))])
    return factor_of


def noise(own_key, shape, spread, reach, split=(), held_as=jnp.bfloat16):
    array = spread * jax.random.normal(own_key, shape, jnp.float32)
    if split:
        array = array * block_scale(own_key, shape, split, -0.22, 0.18)
    return jnp.clip(array, -reach, reach).astype(held_as)


def setup_inputs(seed: int = 0) -> dict:
    key_of = jax.random.split(jax.random.key(seed), 7)
    return {
        "queries": draw_queries(jax.random.fold_in(key_of[6], 71), 0),
        "tile_keys": draw_tile_keys(jax.random.fold_in(key_of[6], 71), 0),
        "values": noise(key_of[2], (VIDEOS, FRAMES, GRID_H, GRID_W, WIDTH), 1.0, 6.0, ((1, 4), (2, 4), (3, 8))),
        "probes": draw_probes(jax.random.fold_in(key_of[6], 71), 0),
        "anchors": draw_anchors(jax.random.fold_in(key_of[6], 71), 0),
        "upstream": noise(key_of[5], (VIDEOS, FRAMES, GRID_H, GRID_W, WIDTH), 1.0, 6.0, ((1, 4), (2, 4), (3, 8))),
    }


NEG_FILL = -1e30


def to_tiles(grid_field):
    videos, frames, grid_rows, grid_cols = grid_field.shape[:4]
    tiled_field = grid_field.reshape(videos * frames, grid_rows // TILE, TILE, grid_cols // TILE, TILE, HEADS, HEAD_DIM)
    tiled_field = tiled_field.transpose(0, 1, 3, 2, 4, 5, 6)
    return tiled_field.reshape(videos * frames, grid_rows // TILE, grid_cols // TILE, TILE * TILE, HEADS, HEAD_DIM)


def from_tiles(tiled_field):
    slabs, tile_rows, tile_cols = tiled_field.shape[:3]
    grid_field = tiled_field.reshape(slabs, tile_rows, tile_cols, TILE, TILE, HEADS, HEAD_DIM)
    grid_field = grid_field.transpose(0, 1, 3, 2, 4, 5, 6)
    return grid_field.reshape(VIDEOS, FRAMES, tile_rows * TILE, tile_cols * TILE, HEADS * HEAD_DIM)


def rounded(full_values):
    return lax.optimization_barrier(full_values.astype(jnp.bfloat16)).astype(jnp.float32)


def neighbourhood(padded, slab_index, row_index, tile_cols):
    window = lax.dynamic_index_in_dim(padded, slab_index, 0, keepdims=False)
    window = lax.dynamic_slice_in_dim(window, row_index, 3, 0)
    pieces = [window[offset_row, offset_col:offset_col + tile_cols] for offset_row in range(3) for offset_col in range(3)]
    return jnp.concatenate(pieces, axis=1)


def near_validity(valid_pad, row_index, tile_cols):
    window = lax.dynamic_slice_in_dim(valid_pad, row_index, 3, 0)
    pieces = [jnp.repeat(window[offset_row, offset_col:offset_col + tile_cols][:, None], TILE * TILE, axis=1) for offset_row in range(3) for offset_col in range(3)]
    return jnp.concatenate(pieces, axis=1)


def spatial_scores(query_tiles, near_keys, near_valid):
    score_scale = HEAD_DIM ** -0.5
    scores = jnp.einsum("nqhd,nkhd->nhqk", query_tiles.astype(jnp.float32), near_keys.astype(jnp.float32)) * score_scale
    return jnp.where(near_valid[:, None, None, :], scores, NEG_FILL)


def spatial_forward(query_tiles, near_keys, near_values, near_valid):
    scores = spatial_scores(query_tiles, near_keys, near_valid)
    row_max = jnp.max(scores, axis=-1, keepdims=True)
    log_total = row_max + jnp.log(jnp.sum(jnp.exp(scores - row_max), axis=-1, keepdims=True))
    weights = jnp.exp(scores - log_total)
    mixed_out = jnp.einsum("nhqk,nkhd->nqhd", rounded(weights), near_values.astype(jnp.float32)).astype(jnp.bfloat16)
    return mixed_out, log_total


def spatial_backward(query_tiles, near_keys, near_values, near_valid, log_total, grad_tiles, mixed_tiles):
    score_scale = HEAD_DIM ** -0.5
    weights = jnp.exp(spatial_scores(query_tiles, near_keys, near_valid) - log_total)
    grad_full = grad_tiles.astype(jnp.float32)
    weight_grads = jnp.einsum("nqhd,nkhd->nhqk", grad_full, near_values.astype(jnp.float32))
    row_term = jnp.einsum("nqhd,nqhd->nhq", grad_full, mixed_tiles.astype(jnp.float32))[..., None]
    score_grads = rounded(weights * (weight_grads - row_term))
    query_grad = (jnp.einsum("nhqk,nkhd->nqhd", score_grads, near_keys.astype(jnp.float32)) * score_scale).astype(jnp.bfloat16)
    key_terms = (jnp.einsum("nhqk,nqhd->nkhd", score_grads, query_tiles.astype(jnp.float32)) * score_scale).astype(jnp.bfloat16)
    value_terms = jnp.einsum("nhqk,nqhd->nkhd", rounded(weights), grad_full).astype(jnp.bfloat16)
    return query_grad, key_terms, value_terms


def add_terms(accumulated, terms, slab_index, row_index, tile_cols):
    zero_index = jnp.zeros((), jnp.int32)
    root = (slab_index, row_index) + (zero_index,) * (accumulated.ndim - 2)
    window = lax.dynamic_slice(accumulated, root, (1, 3) + accumulated.shape[2:])
    pieces = terms.reshape(tile_cols, 9, TILE * TILE, HEADS, HEAD_DIM).astype(accumulated.dtype)
    for offset_row in range(3):
        for offset_col in range(3):
            window = window.at[0, offset_row, offset_col:offset_col + tile_cols].add(pieces[:, offset_row * 3 + offset_col])
    return lax.dynamic_update_slice(accumulated, window, root)


def reference(queries, tile_keys, values, probes, anchors, upstream):
    slabs = VIDEOS * FRAMES
    tile_rows = GRID_H // TILE
    tile_cols = GRID_W // TILE
    tokens = TILE * TILE
    score_scale = HEAD_DIM ** -0.5
    pad_widths = ((0, 0), (1, 1), (1, 1), (0, 0), (0, 0), (0, 0))
    query_tiles = to_tiles(queries)
    key_pad = jnp.pad(to_tiles(tile_keys), pad_widths)
    value_pad = jnp.pad(to_tiles(values), pad_widths)
    valid_pad = jnp.pad(jnp.ones((tile_rows, tile_cols), dtype=jnp.bool_), 1)

    def near_inputs(step_index):
        step_index = step_index.astype(jnp.int32)
        slab_index = step_index // tile_rows
        row_index = step_index % tile_rows
        own_tiles = lax.dynamic_index_in_dim(lax.dynamic_index_in_dim(query_tiles, slab_index, 0, False), row_index, 0, False)
        near_keys = neighbourhood(key_pad, slab_index, row_index, tile_cols)
        near_values = neighbourhood(value_pad, slab_index, row_index, tile_cols)
        near_valid = near_validity(valid_pad, row_index, tile_cols)
        return slab_index, row_index, own_tiles, near_keys, near_values, near_valid

    def forward_row(step_index):
        slab_index, row_index, own_tiles, near_keys, near_values, near_valid = near_inputs(step_index)
        return spatial_forward(own_tiles, near_keys, near_values, near_valid)

    step_list = jnp.arange(slabs * tile_rows, dtype=jnp.int32)
    mixed_rows, log_rows = lax.map(forward_row, step_list)
    mixed_out = from_tiles(mixed_rows.reshape(slabs, tile_rows, tile_cols, tokens, HEADS, HEAD_DIM))

    highest = lax.Precision.HIGHEST

    def heads_view(grid_field):
        return grid_field.reshape(VIDEOS, FRAMES, GRID_H, GRID_W, HEADS, HEAD_DIM).astype(jnp.float32)

    probe_full = heads_view(probes)
    anchor_full = heads_view(anchors)
    mixed_full = heads_view(mixed_out)
    upstream_full = heads_view(upstream)
    time_scores = jnp.einsum("bfxyhd,bgxyhd->bxyhfg", probe_full, anchor_full, precision=highest) * score_scale
    time_weights = jax.nn.softmax(time_scores, axis=-1)
    mixed_grad = jnp.einsum("bxyhfg,bfxyhd->bgxyhd", rounded(time_weights), upstream_full, precision=highest).astype(jnp.bfloat16)
    weight_grads = jnp.einsum("bfxyhd,bgxyhd->bxyhfg", upstream_full, mixed_full, precision=highest)
    row_dot = jnp.sum(time_weights * weight_grads, axis=-1, keepdims=True)
    score_grads = rounded(time_weights * (weight_grads - row_dot))
    full_shape = probes.shape
    probe_grad = (jnp.einsum("bxyhfg,bgxyhd->bfxyhd", score_grads, anchor_full, precision=highest) * score_scale).astype(jnp.bfloat16).reshape(full_shape)
    anchor_grad = (jnp.einsum("bxyhfg,bfxyhd->bgxyhd", score_grads, probe_full, precision=highest) * score_scale).astype(jnp.bfloat16).reshape(full_shape)
    mixed_grad = mixed_grad.reshape(full_shape)

    grad_tiles = to_tiles(mixed_grad)

    def backward_row(step_index, carried):
        query_acc, key_acc, value_acc = carried
        slab_index, row_index, own_tiles, near_keys, near_values, near_valid = near_inputs(step_index)
        own_grad = lax.dynamic_index_in_dim(lax.dynamic_index_in_dim(grad_tiles, slab_index, 0, False), row_index, 0, False)
        log_total = lax.dynamic_index_in_dim(log_rows, step_index.astype(jnp.int32), 0, False)
        own_mixed = lax.dynamic_index_in_dim(mixed_rows, step_index.astype(jnp.int32), 0, False)
        query_part, key_terms, value_terms = spatial_backward(own_tiles, near_keys, near_values, near_valid, log_total, own_grad, own_mixed)
        zero_index = jnp.zeros((), jnp.int32)
        root = (slab_index, row_index, zero_index, zero_index, zero_index, zero_index)
        query_acc = lax.dynamic_update_slice(query_acc, query_part[None, None], root)
        key_acc = add_terms(key_acc, key_terms, slab_index, row_index, tile_cols)
        value_acc = add_terms(value_acc, value_terms, slab_index, row_index, tile_cols)
        return query_acc, key_acc, value_acc

    query_init = jnp.zeros((slabs, tile_rows, tile_cols, tokens, HEADS, HEAD_DIM), jnp.bfloat16)
    pad_init = jnp.zeros((slabs, tile_rows + 2, tile_cols + 2, tokens, HEADS, HEAD_DIM), jnp.float32)
    query_acc, key_acc, value_acc = lax.fori_loop(0, slabs * tile_rows, backward_row, (query_init, pad_init, pad_init))
    query_grad = from_tiles(query_acc)
    key_grad = from_tiles(key_acc[:, 1:-1, 1:-1].astype(jnp.bfloat16))
    value_grad = from_tiles(value_acc[:, 1:-1, 1:-1].astype(jnp.bfloat16))
    return (query_grad, key_grad, value_grad, probe_grad, anchor_grad)
```

```python
import functools

import jax
import jax.numpy as jnp
from jax import lax
from jax.experimental import pallas as pl
from jax.experimental.pallas import tpu as pltpu
from jax.sharding import PartitionSpec as P

HEADS = 12
HEAD_DIM = 128
PARTS = 4
GROUP = HEADS // PARTS
ROWS = 4
BIG = 1e30
SCALE = HEAD_DIM ** (-0.5)
LOG2E = 1.4426950408889634
BASE2 = SCALE * LOG2E

NT = (((1,), (1,)), ((), ()))
NN = (((1,), (0,)), ((), ()))
TN = (((0,), (0,)), ((), ()))


def dot(a, b, dims):
    return lax.dot_general(a, b, dims, preferred_element_type=jnp.float32)


def params():
    return pltpu.CompilerParams(vmem_limit_bytes=56 * 1024 * 1024)


def cost(flops, bytes_accessed, transcendentals=0):
    return pl.CostEstimate(
        flops=flops, bytes_accessed=bytes_accessed, transcendentals=transcendentals
    )


def pack(arrays):
    count = len(arrays)
    tokens = arrays[0].shape[0]

    def kernel(*refs):
        out = refs[-1]
        for a in range(count):
            for h in range(GROUP):
                out[0, h, a] = refs[a][:, h * HEAD_DIM : (h + 1) * HEAD_DIM]

    total = count * tokens * HEADS * HEAD_DIM
    return pl.pallas_call(
        kernel,
        grid=(PARTS,),
        in_specs=[pl.BlockSpec((tokens, GROUP * HEAD_DIM), lambda i: (0, i))] * count,
        out_specs=pl.BlockSpec((1, GROUP, count, tokens, HEAD_DIM), lambda i: (i, 0, 0, 0, 0)),
        out_shape=jax.ShapeDtypeStruct(
            (PARTS, GROUP, count, tokens, HEAD_DIM), arrays[0].dtype
        ),
        cost_estimate=cost(0, 4 * total),
        compiler_params=params(),
    )(*arrays)


def unpack(block):
    count, tokens = block.shape[2:4]

    def kernel(block_ref, *outs):
        for a in range(count):
            for h in range(GROUP):
                outs[a][:, h * HEAD_DIM : (h + 1) * HEAD_DIM] = block_ref[0, h, a]

    total = count * tokens * HEADS * HEAD_DIM
    return pl.pallas_call(
        kernel,
        grid=(PARTS,),
        in_specs=[
            pl.BlockSpec((1, GROUP, count, tokens, HEAD_DIM), lambda i: (i, 0, 0, 0, 0))
        ],
        out_specs=[pl.BlockSpec((tokens, GROUP * HEAD_DIM), lambda i: (0, i))] * count,
        out_shape=[jax.ShapeDtypeStruct((tokens, HEADS * HEAD_DIM), block.dtype)] * count,
        cost_estimate=cost(0, 4 * total),
        compiler_params=params(),
    )(block)


def near_rows(row):
    return range(max(row - 1, 0), min(row + 2, ROWS))


def forward_kernel(bad_ref, q_ref, kl_ref, kc_ref, kr_ref, o_ref, lse_ref):
    bads = (bad_ref[0], jnp.float32(0.0), bad_ref[1])
    sides = (kl_ref, kc_ref, kr_ref)
    for b in range(ROWS):
        query = q_ref[b, 0, 0]
        scores = []
        for side in range(3):
            for u in near_rows(b):
                scores.append((side, u, dot(sides[side][u, 0, 0], query, NT)))
        top = None
        for side in range(3):
            local = None
            for at, _, s in scores:
                if at == side:
                    one = jnp.max(s, axis=0, keepdims=True)
                    local = one if local is None else jnp.maximum(local, one)
            local = local - bads[side]
            top = local if top is None else jnp.maximum(top, local)
        top = top * BASE2
        total = None
        mixed = None
        for side, u, s in scores:
            p = jnp.exp2(s * BASE2 - (top + bads[side]))
            one = jnp.sum(p, axis=0, keepdims=True)
            total = one if total is None else total + one
            term = dot(sides[side][u, 0, 1], p.astype(jnp.bfloat16), TN)
            mixed = term if mixed is None else mixed + term
        mixed = mixed * (1.0 / total)
        o_ref[b, 0, 0] = mixed.T.astype(jnp.bfloat16)
        lse_ref[0, b] = top + jnp.log2(total)


def column_spec(count, tokens):
    return pl.BlockSpec((ROWS, 1, count, tokens, HEAD_DIM), lambda h: (0, h, 0, 0, 0))


def attend_forward(bad, q, kv_left, kv, kv_right):
    tokens = q.shape[3]
    group = q.shape[1]
    pairs = 3 * 10 * group
    return pl.pallas_call(
        forward_kernel,
        grid=(group,),
        in_specs=[pl.BlockSpec(memory_space=pltpu.SMEM), column_spec(1, tokens)]
        + [column_spec(2, tokens)] * 3,
        out_specs=[
            column_spec(1, tokens),
            pl.BlockSpec((1, ROWS, 1, tokens), lambda h: (h, 0, 0, 0)),
        ],
        out_shape=[
            jax.ShapeDtypeStruct(q.shape, jnp.bfloat16),
            jax.ShapeDtypeStruct((group, ROWS, 1, tokens), jnp.float32),
        ],
        cost_estimate=cost(
            4 * pairs * tokens * tokens * HEAD_DIM, 8 * q.size * 2, pairs * tokens * tokens
        ),
        compiler_params=params(),
    )(bad, q, kv_left, kv, kv_right)


def backward_kernel(
    bad_ref,
    q_ref,
    kl_ref,
    kc_ref,
    kr_ref,
    do_ref,
    o_ref,
    lse_ref,
    dq_ref,
    dl_ref,
    dc_ref,
    dr_ref,
    dqt_ref,
    row_ref,
):
    bads = (bad_ref[0], jnp.float32(0.0), bad_ref[1])
    sides = (kl_ref, kc_ref, kr_ref)
    outs = (dl_ref, dc_ref, dr_ref)
    for b in range(ROWS):
        product = do_ref[b, 0, 0].astype(jnp.float32) * o_ref[b, 0, 0].astype(jnp.float32)
        row_ref[b] = jnp.sum(product.T, axis=0, keepdims=True)
    seen = set()
    for side in (0, 2, 1):
        for u in range(ROWS):
            key = sides[side][u, 0, 0]
            value = sides[side][u, 0, 1]
            dk = None
            dv = None
            for b in near_rows(u):
                query = q_ref[b, 0, 0]
                grad = do_ref[b, 0, 0]
                s = dot(key, query, NT)
                p = jnp.exp2(s * BASE2 - (lse_ref[0, b] + bads[side]))
                e = dot(value, grad, NT)
                g = (p * (e - row_ref[b])).astype(jnp.bfloat16)
                tv = dot(p.astype(jnp.bfloat16), grad, NN)
                tk = dot(g, query, NN)
                tq = dot(key, g, TN)
                dv = tv if dv is None else dv + tv
                dk = tk if dk is None else dk + tk
                if b in seen:
                    dqt_ref[b] += tq
                else:
                    seen.add(b)
                    dqt_ref[b] = tq
            outs[side][u, 0, 0] = (dk * SCALE).astype(outs[side].dtype)
            outs[side][u, 0, 1] = dv.astype(outs[side].dtype)
    for b in range(ROWS):
        dq_ref[b, 0, 0] = (dqt_ref[b] * SCALE).T.astype(jnp.bfloat16)


def attend_backward(bad, q, kv_left, kv, kv_right, grad, mixed, lse):
    tokens = q.shape[3]
    group = q.shape[1]
    pairs = 3 * 10 * group
    return pl.pallas_call(
        backward_kernel,
        grid=(group,),
        in_specs=[pl.BlockSpec(memory_space=pltpu.SMEM), column_spec(1, tokens)]
        + [column_spec(2, tokens)] * 3
        + [column_spec(1, tokens)] * 2
        + [pl.BlockSpec((1, ROWS, 1, tokens), lambda h: (h, 0, 0, 0))],
        out_specs=[column_spec(1, tokens)] + [column_spec(2, tokens)] * 3,
        out_shape=[
            jax.ShapeDtypeStruct(q.shape, jnp.bfloat16),
            jax.ShapeDtypeStruct(kv.shape, jnp.bfloat16),
            jax.ShapeDtypeStruct(kv.shape, jnp.float32),
            jax.ShapeDtypeStruct(kv.shape, jnp.bfloat16),
        ],
        scratch_shapes=[
            pltpu.VMEM((ROWS, HEAD_DIM, tokens), jnp.float32),
            pltpu.VMEM((ROWS, 1, tokens), jnp.float32),
        ],
        cost_estimate=cost(
            10 * pairs * tokens * tokens * HEAD_DIM, 20 * q.size * 2, pairs * tokens * tokens
        ),
        compiler_params=params(),
    )(bad, q, kv_left, kv, kv_right, grad, mixed, lse)


def lane_dots(a, b, ones):
    product = a * b
    high = product.astype(jnp.bfloat16)
    low = (product - high.astype(jnp.float32)).astype(jnp.bfloat16)
    return dot(high, ones, NN) + dot(low, ones, NN)


def temporal_weights(probes, anchors, ones):
    weights = []
    for f in range(PARTS):
        scores = [lane_dots(probes[f], anchors[g], ones) * SCALE for g in range(PARTS)]
        top = functools.reduce(jnp.maximum, scores)
        shifted = [jnp.exp(s - top) for s in scores]
        inverse = 1.0 / functools.reduce(jnp.add, shifted)
        weights.append([s * inverse for s in shifted])
    return weights


def rounded(x):
    return x.astype(jnp.bfloat16).astype(jnp.float32)


def temporal_forward_kernel(pau_ref, out_ref):
    ones = jnp.ones((HEAD_DIM, HEAD_DIM), jnp.bfloat16)
    parts = [[pau_ref[f, 0, t].astype(jnp.float32) for f in range(PARTS)] for t in range(3)]
    weights = temporal_weights(parts[0], parts[1], ones)
    for g in range(PARTS):
        terms = [rounded(weights[f][g]) * parts[2][f] for f in range(PARTS)]
        out_ref[g, 0, 0] = functools.reduce(jnp.add, terms).astype(jnp.bfloat16)


def temporal_backward_kernel(pau_ref, mixed_ref, out_ref):
    ones = jnp.ones((HEAD_DIM, HEAD_DIM), jnp.bfloat16)
    parts = [[pau_ref[f, 0, t].astype(jnp.float32) for f in range(PARTS)] for t in range(3)]
    mixed = [mixed_ref[g, 0, 0].astype(jnp.float32) for g in range(PARTS)]
    weights = temporal_weights(parts[0], parts[1], ones)
    anchor_grads = [None] * PARTS
    for f in range(PARTS):
        grads = [lane_dots(parts[2][f], mixed[g], ones) for g in range(PARTS)]
        row = functools.reduce(jnp.add, [w * c for w, c in zip(weights[f], grads)])
        scores = [rounded(w * (c - row)) for w, c in zip(weights[f], grads)]
        probe = functools.reduce(jnp.add, [s * parts[1][g] for g, s in enumerate(scores)])
        out_ref[f, 0, 0] = (probe * SCALE).astype(jnp.bfloat16)
        for g in range(PARTS):
            term = scores[g] * parts[0][f]
            anchor_grads[g] = term if f == 0 else anchor_grads[g] + term
    for g in range(PARTS):
        out_ref[g, 0, 1] = (anchor_grads[g] * SCALE).astype(jnp.bfloat16)


def temporal_call(kernel, arrays, count_out):
    _, group, _, tokens, _ = arrays[0].shape
    rows = 64
    pairs = 16 * group * tokens

    def spec(count):
        return pl.BlockSpec(
            (PARTS, 1, count, rows, HEAD_DIM), lambda h, i: (0, h, 0, i, 0)
        )

    return pl.pallas_call(
        kernel,
        grid=(group, tokens // rows),
        in_specs=[spec(a.shape[2]) for a in arrays],
        out_specs=spec(count_out),
        out_shape=jax.ShapeDtypeStruct(
            (PARTS, group, count_out, tokens, HEAD_DIM), jnp.bfloat16
        ),
        cost_estimate=cost(
            pairs * 4 * HEAD_DIM * HEAD_DIM,
            2 * sum(a.size for a in arrays),
            pairs * HEAD_DIM,
        ),
        compiler_params=params(),
    )(*arrays)


def swap(x, axis):
    return lax.all_to_all(x, axis, split_axis=0, concat_axis=0, tiled=True)


def shift_right(x):
    count = lax.axis_size("wa")
    return lax.ppermute(x, "wa", [(i, i + 1) for i in range(count - 1)])


def shift_left(x):
    count = lax.axis_size("wa")
    return lax.ppermute(x, "wa", [(i + 1, i) for i in range(count - 1)])


def shards(queries, tile_keys, values, probes, anchors, upstream):
    shape = queries.shape
    tokens = shape[2] * shape[3]

    def flat(x):
        return x.reshape(tokens, shape[-1])

    place = lax.axis_index("wa")
    bad = jnp.stack([place == 0, place == lax.axis_size("wa") - 1]).astype(jnp.float32) * BIG

    kv = swap(pack([flat(tile_keys), flat(values)]), "ha")
    pau = swap(pack([flat(probes), flat(anchors), flat(upstream)]), "tm")
    q = swap(pack([flat(queries)]), "ha")
    kv_left = shift_right(kv)
    kv_right = shift_left(kv)
    grad = swap(swap(temporal_call(temporal_forward_kernel, [pau], 1), "tm"), "ha")
    mixed, lse = attend_forward(bad, q, kv_left, kv, kv_right)
    mixed_back = swap(swap(mixed, "ha"), "tm")
    dq, to_left, own, to_right = attend_backward(
        bad, q, kv_left, kv, kv_right, grad, mixed, lse
    )
    times = swap(temporal_call(temporal_backward_kernel, [pau, mixed_back], 2), "tm")
    query_grad = unpack(swap(dq, "ha"))[0]
    summed = (
        own
        + shift_right(to_right).astype(jnp.float32)
        + shift_left(to_left).astype(jnp.float32)
    ).astype(jnp.bfloat16)
    key_grad, value_grad = unpack(swap(summed, "ha"))
    probe_grad, anchor_grad = unpack(times)
    outs = (query_grad, key_grad, value_grad, probe_grad, anchor_grad)
    return tuple(x.reshape(shape) for x in outs)


def solution(mesh):
    spec = P(None, "tm", "ha", "wa", None)
    return jax.shard_map(
        shards,
        mesh=mesh,
        in_specs=(spec,) * 6,
        out_specs=(spec,) * 5,
        check_vma=False,
    )
```

```python
import functools

import jax
import jax.numpy as jnp
from jax import lax
from jax.experimental import pallas as pl
from jax.experimental.pallas import tpu as pltpu
from jax.sharding import PartitionSpec as P

HEADS = 12
HEAD_DIM = 128
PARTS = 4
GROUP = HEADS // PARTS
ROWS = 4
BIG = 1e30
SCALE = HEAD_DIM ** (-0.5)
LOG2E = 1.4426950408889634
BASE2 = SCALE * LOG2E

NT = (((1,), (1,)), ((), ()))
NN = (((1,), (0,)), ((), ()))
TN = (((0,), (0,)), ((), ()))


def dot(a, b, dims):
    return lax.dot_general(a, b, dims, preferred_element_type=jnp.float32)


def params():
    return pltpu.CompilerParams(vmem_limit_bytes=56 * 1024 * 1024)


def cost(microseconds):
    return pl.CostEstimate(
        flops=int(microseconds * 1e9), bytes_accessed=1024, transcendentals=0
    )


def move(inputs, out_shapes, plan, axis=None, after=(), told=0.1):
    first = len(inputs) + len(after)

    def kernel(*refs):
        ins = refs[: len(inputs)]
        outs = refs[first:]
        me = 0 if axis is None else lax.axis_index(axis)
        for i, at, o, to in plan(me):
            outs[o][to] = ins[i][at]

    return pl.pallas_call(
        kernel,
        in_specs=[pl.BlockSpec(memory_space=pltpu.VMEM)] * len(inputs)
        + [pl.BlockSpec(memory_space=pl.ANY)] * len(after),
        out_specs=[pl.BlockSpec(memory_space=pltpu.VMEM)] * len(out_shapes),
        out_shape=out_shapes,
        cost_estimate=cost(told),
        compiler_params=params(),
    )(*inputs, *after)


def columns(group, head):
    start = (group * GROUP + head) * HEAD_DIM
    if not isinstance(start, int):
        start = pl.multiple_of(start, HEAD_DIM)
    return (slice(None), pl.ds(start, HEAD_DIM))


def bf16(*shape):
    return jax.ShapeDtypeStruct(shape, jnp.bfloat16)


def pack(arrays, after=()):
    tokens = arrays[0].shape[0]
    cells = [(a, d, h) for d in range(PARTS) for h in range(GROUP) for a in range(len(arrays))]
    return move(
        arrays,
        [bf16(PARTS, GROUP, len(arrays), tokens, HEAD_DIM)],
        lambda me: [(a, columns(d, h), 0, (d, h, a)) for a, d, h in cells],
        after=after,
    )[0]


def pack_partners(arrays):
    tokens = arrays[0].shape[0]
    cells = [(a, s, h) for s in range(PARTS) for h in range(GROUP) for a in range(len(arrays))]
    return move(
        arrays,
        [bf16(GROUP, len(arrays), tokens, HEAD_DIM)] * PARTS,
        lambda me: [(a, columns(me ^ s, h), s, (h, a)) for a, s, h in cells],
        "tm",
    )


def unpack_partners(chunks):
    _, count, tokens, _ = chunks[0].shape
    cells = [(a, s, h) for s in range(PARTS) for h in range(GROUP) for a in range(count)]
    return move(
        chunks,
        [bf16(tokens, HEADS * HEAD_DIM)] * count,
        lambda me: [(s, (h, a), a, columns(me ^ s, h)) for a, s, h in cells],
        "tm",
        told=100,
    )


def join_partners(chunks):
    return move(
        chunks,
        [bf16(PARTS, *chunks[0].shape)],
        lambda me: [(s, (slice(None),), 0, (me ^ s,)) for s in range(PARTS)],
        "tm",
    )[0]


def split_partners(block):
    return move(
        [block],
        [bf16(*block.shape[1:])] * PARTS,
        lambda me: [(0, (me ^ s,), s, (slice(None),)) for s in range(PARTS)],
        "tm",
    )


def unpack_heads(blocks):
    count, tokens = blocks[0].shape[2:4]
    cells = [(a, d, h) for h in range(GROUP) for d in range(PARTS) for a in range(count)]
    return move(
        blocks,
        [bf16(tokens, HEADS * HEAD_DIM)] * count,
        lambda me: [(h, (d, 0, a), a, columns(d, h)) for a, d, h in cells],
    )


def trade(chunks):
    out = [chunks[0]]
    for s in range(1, PARTS):
        out.append(lax.ppermute(chunks[s], "tm", [(i, i ^ s) for i in range(PARTS)]))
    return out


def near_rows(row):
    return range(max(row - 1, 0), min(row + 2, ROWS))


def forward_kernel(bad_ref, q_ref, kl_ref, kc_ref, kr_ref, o_ref, lse_ref):
    bads = (bad_ref[0], jnp.float32(0.0), bad_ref[1])
    sides = (kl_ref, kc_ref, kr_ref)
    for b in range(ROWS):
        query = q_ref[b, 0, 0]
        scores = []
        for side in range(3):
            for u in near_rows(b):
                scores.append((side, u, dot(sides[side][u, 0, 0], query, NT)))
        top = None
        for side in range(3):
            local = None
            for at, _, s in scores:
                if at == side:
                    one = jnp.max(s, axis=0, keepdims=True)
                    local = one if local is None else jnp.maximum(local, one)
            local = local - bads[side]
            top = local if top is None else jnp.maximum(top, local)
        top = top * BASE2
        total = None
        mixed = None
        for side, u, s in scores:
            p = jnp.exp2(s * BASE2 - (top + bads[side]))
            one = jnp.sum(p, axis=0, keepdims=True)
            total = one if total is None else total + one
            term = dot(sides[side][u, 0, 1], p.astype(jnp.bfloat16), TN)
            mixed = term if mixed is None else mixed + term
        mixed = mixed * (1.0 / total)
        o_ref[b, 0, 0] = mixed.T.astype(jnp.bfloat16)
        lse_ref[0, b] = top + jnp.log2(total)


def column_spec(count, tokens):
    return pl.BlockSpec((ROWS, 1, count, tokens, HEAD_DIM), lambda h: (0, h, 0, 0, 0))


def attend_forward(bad, q, kv_left, kv, kv_right):
    tokens = q.shape[3]
    group = q.shape[1]
    return pl.pallas_call(
        forward_kernel,
        grid=(group,),
        in_specs=[pl.BlockSpec(memory_space=pltpu.SMEM), column_spec(1, tokens)]
        + [column_spec(2, tokens)] * 3,
        out_specs=[
            column_spec(1, tokens),
            pl.BlockSpec((1, ROWS, 1, tokens), lambda h: (h, 0, 0, 0)),
        ],
        out_shape=[
            jax.ShapeDtypeStruct(q.shape, jnp.bfloat16),
            jax.ShapeDtypeStruct((group, ROWS, 1, tokens), jnp.float32),
        ],
        cost_estimate=cost(100),
        compiler_params=params(),
    )(bad, q, kv_left, kv, kv_right)


def backward_kernel(
    bad_ref,
    q_ref,
    kl_ref,
    kc_ref,
    kr_ref,
    do_ref,
    o_ref,
    lse_ref,
    _,
    dq_ref,
    dl_ref,
    dc_ref,
    dr_ref,
    dqt_ref,
    row_ref,
):
    bads = (bad_ref[0], jnp.float32(0.0), bad_ref[1])
    sides = (kl_ref, kc_ref, kr_ref)
    outs = (dl_ref, dc_ref, dr_ref)
    for b in range(ROWS):
        product = do_ref[b, 0, 0].astype(jnp.float32) * o_ref[b, 0, 0].astype(jnp.float32)
        row_ref[b] = jnp.sum(product.T, axis=0, keepdims=True)
    seen = set()
    for side in (0, 2, 1):
        for u in range(ROWS):
            key = sides[side][u, 0, 0]
            value = sides[side][u, 0, 1]
            dk = None
            dv = None
            for b in near_rows(u):
                query = q_ref[b, 0, 0]
                grad = do_ref[b, 0, 0]
                s = dot(key, query, NT)
                p = jnp.exp2(s * BASE2 - (lse_ref[0, b] + bads[side]))
                e = dot(value, grad, NT)
                g = (p * (e - row_ref[b])).astype(jnp.bfloat16)
                tv = dot(p.astype(jnp.bfloat16), grad, NN)
                tk = dot(g, query, NN)
                tq = dot(key, g, TN)
                dv = tv if dv is None else dv + tv
                dk = tk if dk is None else dk + tk
                if b in seen:
                    dqt_ref[b] += tq
                else:
                    seen.add(b)
                    dqt_ref[b] = tq
            outs[side][u, 0, 0] = (dk * SCALE).astype(outs[side].dtype)
            outs[side][u, 0, 1] = dv.astype(outs[side].dtype)
    for b in range(ROWS):
        dq_ref[b, 0, 0] = (dqt_ref[b] * SCALE).T.astype(jnp.bfloat16)


def head_spec(head, count, tokens):
    return pl.BlockSpec((ROWS, 1, count, tokens, HEAD_DIM), lambda i: (0, head, 0, 0, 0))


def attend_backward(head, bad, q, kv_left, kv, kv_right, grad, mixed, lse, after):
    tokens = q.shape[3]
    return pl.pallas_call(
        backward_kernel,
        grid=(1,),
        in_specs=[pl.BlockSpec(memory_space=pltpu.SMEM), head_spec(head, 1, tokens)]
        + [head_spec(head, 2, tokens)] * 3
        + [head_spec(head, 1, tokens)] * 2
        + [pl.BlockSpec((1, ROWS, 1, tokens), lambda i: (head, 0, 0, 0))]
        + [pl.BlockSpec(memory_space=pl.ANY)],
        out_specs=[head_spec(0, 1, tokens)] + [head_spec(0, 2, tokens)] * 3,
        out_shape=[bf16(ROWS, 1, 1, tokens, HEAD_DIM)]
        + [bf16(ROWS, 1, 2, tokens, HEAD_DIM)] * 3,
        scratch_shapes=[
            pltpu.VMEM((ROWS, HEAD_DIM, tokens), jnp.float32),
            pltpu.VMEM((ROWS, 1, tokens), jnp.float32),
        ],
        cost_estimate=cost(100),
        compiler_params=params(),
    )(bad, q, kv_left, kv, kv_right, grad, mixed, lse, after)


def total_kernel(dq_ref, own_ref, a_ref, b_ref, _, out_ref):
    out_ref[0, 0, 0] = dq_ref[0, 0, 0]
    for t in range(2):
        total = own_ref[0, 0, t].astype(jnp.float32) + a_ref[0, 0, t].astype(jnp.float32)
        out_ref[0, 0, 1 + t] = (total + b_ref[0, 0, t].astype(jnp.float32)).astype(jnp.bfloat16)


def totals(dq, own, a, b, after):
    tokens = dq.shape[3]

    def spec(count):
        return pl.BlockSpec((1, 1, count, tokens, HEAD_DIM), lambda i: (i, 0, 0, 0, 0))

    return pl.pallas_call(
        total_kernel,
        grid=(ROWS,),
        in_specs=[spec(1), spec(2), spec(2), spec(2), pl.BlockSpec(memory_space=pl.ANY)],
        out_specs=spec(3),
        out_shape=bf16(ROWS, 1, 3, tokens, HEAD_DIM),
        cost_estimate=cost(0.1),
        compiler_params=params(),
    )(dq, own, a, b, after)


def lane_sums(products):
    rows = products[0].shape[0]
    product = jnp.concatenate(products, axis=0)
    high = product.astype(jnp.bfloat16)
    low = (product - high.astype(jnp.float32)).astype(jnp.bfloat16)
    ones = jnp.ones((2 * HEAD_DIM, HEAD_DIM), jnp.bfloat16)
    sums = dot(jnp.concatenate([high, low], axis=1), ones, NN)
    return [sums[i * rows : (i + 1) * rows] for i in range(len(products))]


def temporal_weights(probes, anchors):
    scores = lane_sums([p * a for p in probes for a in anchors])
    weights = []
    for f in range(PARTS):
        row = [s * SCALE for s in scores[f * PARTS : (f + 1) * PARTS]]
        top = functools.reduce(jnp.maximum, row)
        shifted = [jnp.exp(s - top) for s in row]
        inverse = 1.0 / functools.reduce(jnp.add, shifted)
        weights.append([s * inverse for s in shifted])
    return weights


def rounded(x):
    return x.astype(jnp.bfloat16).astype(jnp.float32)


def temporal_forward_kernel(*refs):
    ins, outs = refs[:PARTS], refs[PARTS:]
    parts = [[ref[0, t].astype(jnp.float32) for ref in ins] for t in range(3)]
    weights = temporal_weights(parts[0], parts[1])
    for g in range(PARTS):
        terms = [rounded(weights[f][g]) * parts[2][f] for f in range(PARTS)]
        outs[g][0, 0] = functools.reduce(jnp.add, terms).astype(jnp.bfloat16)


def temporal_backward_kernel(*refs):
    ins, mixed_refs, outs = refs[:PARTS], refs[PARTS : 2 * PARTS], refs[-PARTS:]
    parts = [[ref[0, t].astype(jnp.float32) for ref in ins] for t in range(3)]
    mixed = [ref[0, 0].astype(jnp.float32) for ref in mixed_refs]
    weights = temporal_weights(parts[0], parts[1])
    sums = lane_sums([u * m for u in parts[2] for m in mixed])
    anchor_grads = [None] * PARTS
    for f in range(PARTS):
        grads = sums[f * PARTS : (f + 1) * PARTS]
        row = functools.reduce(jnp.add, [w * c for w, c in zip(weights[f], grads)])
        scores = [rounded(w * (c - row)) for w, c in zip(weights[f], grads)]
        probe = functools.reduce(jnp.add, [s * parts[1][g] for g, s in enumerate(scores)])
        outs[f][0, 0] = (probe * SCALE).astype(jnp.bfloat16)
        for g in range(PARTS):
            term = scores[g] * parts[0][f]
            anchor_grads[g] = term if f == 0 else anchor_grads[g] + term
    for g in range(PARTS):
        outs[g][0, 1] = (anchor_grads[g] * SCALE).astype(jnp.bfloat16)


def temporal_call(kernel, arrays, count_out, told, after=()):
    group, _, tokens, _ = arrays[0].shape
    rows = 128

    def spec(count):
        return pl.BlockSpec((1, count, rows, HEAD_DIM), lambda h, i: (h, 0, i, 0))

    return pl.pallas_call(
        kernel,
        grid=(group, tokens // rows),
        in_specs=[spec(a.shape[1]) for a in arrays]
        + [pl.BlockSpec(memory_space=pl.ANY)] * len(after),
        out_specs=[spec(count_out)] * PARTS,
        out_shape=[bf16(group, count_out, tokens, HEAD_DIM)] * PARTS,
        cost_estimate=cost(told),
        compiler_params=params(),
    )(*arrays, *after)


def swap(x, axis):
    return lax.all_to_all(x, axis, split_axis=0, concat_axis=0, tiled=True)


def shift_right(x):
    count = lax.axis_size("wa")
    return lax.ppermute(x, "wa", [(i, i + 1) for i in range(count - 1)])


def shift_left(x):
    count = lax.axis_size("wa")
    return lax.ppermute(x, "wa", [(i + 1, i) for i in range(count - 1)])


def shards(queries, tile_keys, values, probes, anchors, upstream):
    shape = queries.shape
    tokens = shape[2] * shape[3]

    def flat(x):
        return x.reshape(tokens, shape[-1])

    place = lax.axis_index("wa")
    bad = jnp.stack([place == 0, place == lax.axis_size("wa") - 1]).astype(jnp.float32) * BIG

    pau_sent = pack_partners([flat(probes), flat(anchors), flat(upstream)])
    pau = trade(pau_sent)
    kv = swap(pack([flat(tile_keys), flat(values)], [pau_sent[1]]), "ha")
    kv_left = shift_right(kv)
    kv_right = shift_left(kv)
    q = swap(pack([flat(queries)], [kv]), "ha")
    grad_parts = trade(temporal_call(temporal_forward_kernel, pau, 1, 100))
    grad = swap(join_partners(grad_parts), "ha")
    mixed, lse = attend_forward(bad, q, kv_left, kv, kv_right)
    mixed_sent = split_partners(swap(mixed, "ha"))
    mixed_parts = trade(mixed_sent)
    def backward(head, after):
        dq, to_left, own, to_right = attend_backward(
            head, bad, q, kv_left, kv, kv_right, grad, mixed, lse, after
        )
        return dq, own, shift_right(to_right), shift_left(to_left)

    zero = backward(0, q)
    one = backward(1, mixed_sent[0])
    summed = [totals(*zero, one[0])]
    times_sent = temporal_call(
        temporal_backward_kernel, pau + mixed_parts, 2, 100, [summed[0]]
    )
    probe_grad, anchor_grad = unpack_partners(trade(times_sent))
    two = backward(2, times_sent[0])
    summed += [totals(*one, two[0]), totals(*two, probe_grad)]
    summed = [swap(x, "ha") for x in summed]
    query_grad, key_grad, value_grad = unpack_heads(summed)
    outs = (query_grad, key_grad, value_grad, probe_grad, anchor_grad)
    return tuple(x.reshape(shape) for x in outs)


def solution(mesh):
    spec = P(None, "tm", "ha", "wa", None)
    return jax.shard_map(
        shards,
        mesh=mesh,
        in_specs=(spec,) * 6,
        out_specs=(spec,) * 5,
        check_vma=False,
    )
```

```python
import functools

import jax
import jax.numpy as jnp
from jax import lax
from jax.experimental import pallas as pl
from jax.experimental.pallas import tpu as pltpu
from jax.sharding import PartitionSpec as P

HEADS = 12
HEAD_DIM = 128
PARTS = 4
GROUP = HEADS // PARTS
ROWS = 4
BIG = 1e30
SCALE = HEAD_DIM ** (-0.5)
LOG2E = 1.4426950408889634
BASE2 = SCALE * LOG2E

NT = (((1,), (1,)), ((), ()))
NN = (((1,), (0,)), ((), ()))
TN = (((0,), (0,)), ((), ()))


def dot(a, b, dims):
    return lax.dot_general(a, b, dims, preferred_element_type=jnp.float32)


def params():
    return pltpu.CompilerParams(vmem_limit_bytes=63 * 1024 * 1024)


def cost(microseconds):
    return pl.CostEstimate(
        flops=int(microseconds * 1e9), bytes_accessed=1024, transcendentals=0
    )


def move(inputs, out_shapes, plan, axis=None, after=(), told=0.1):
    first = len(inputs) + len(after)

    def kernel(*refs):
        ins = refs[: len(inputs)]
        outs = refs[first:]
        me = 0 if axis is None else lax.axis_index(axis)
        for i, at, o, to in plan(me):
            outs[o][to] = ins[i][at]

    return pl.pallas_call(
        kernel,
        in_specs=[pl.BlockSpec(memory_space=pltpu.VMEM)] * len(inputs)
        + [pl.BlockSpec(memory_space=pl.ANY)] * len(after),
        out_specs=[pl.BlockSpec(memory_space=pltpu.VMEM)] * len(out_shapes),
        out_shape=out_shapes,
        cost_estimate=cost(told),
        compiler_params=params(),
    )(*inputs, *after)


def columns(group, head):
    start = (group * GROUP + head) * HEAD_DIM
    if not isinstance(start, int):
        start = pl.multiple_of(start, HEAD_DIM)
    return (slice(None), pl.ds(start, HEAD_DIM))


def bf16(*shape):
    return jax.ShapeDtypeStruct(shape, jnp.bfloat16)


def pack(arrays, after=()):
    tokens = arrays[0].shape[0]
    cells = [(a, d, h) for d in range(PARTS) for h in range(GROUP) for a in range(len(arrays))]
    return move(
        arrays,
        [bf16(PARTS, GROUP, len(arrays), tokens, HEAD_DIM)],
        lambda me: [(a, columns(d, h), 0, (d, h, a)) for a, d, h in cells],
        after=after,
    )[0]


def pack_partners(arrays, after=()):
    tokens = arrays[0].shape[0]
    cells = [(a, s, h) for s in range(PARTS) for h in range(GROUP) for a in range(len(arrays))]
    return move(
        arrays,
        [bf16(GROUP, len(arrays), tokens, HEAD_DIM)] * PARTS,
        lambda me: [(a, columns(me ^ s, h), s, (h, a)) for a, s, h in cells],
        "tm",
        after,
    )


def unpack_partners(chunks, after):
    _, count, tokens, _ = chunks[0].shape
    cells = [(a, s, h) for s in range(PARTS) for h in range(GROUP) for a in range(count)]
    return move(
        chunks,
        [bf16(tokens, HEADS * HEAD_DIM)] * count,
        lambda me: [(s, (h, a), a, columns(me ^ s, h)) for a, s, h in cells],
        "tm",
        after,
        told=100,
    )


def join_partners(chunks):
    return move(
        chunks,
        [bf16(PARTS, *chunks[0].shape)],
        lambda me: [(s, (slice(None),), 0, (me ^ s,)) for s in range(PARTS)],
        "tm",
    )[0]


def split_partners(block):
    return move(
        [block],
        [bf16(*block.shape[1:])] * PARTS,
        lambda me: [(0, (me ^ s,), s, (slice(None),)) for s in range(PARTS)],
        "tm",
    )


def unpack_heads(blocks):
    count, tokens = blocks[0].shape[2:4]
    heads = [(n, i) for n, block in enumerate(blocks) for i in range(block.shape[1])]
    cells = [(a, d, h) for h in range(GROUP) for d in range(PARTS) for a in range(count)]
    return move(
        blocks,
        [bf16(tokens, HEADS * HEAD_DIM)] * count,
        lambda me: [
            (heads[h][0], (d, heads[h][1], a), a, columns(d, h)) for a, d, h in cells
        ],
    )


def trade(chunks):
    out = [chunks[0]]
    for s in range(1, PARTS):
        out.append(lax.ppermute(chunks[s], "tm", [(i, i ^ s) for i in range(PARTS)]))
    return out


def near_rows(row):
    return range(max(row - 1, 0), min(row + 2, ROWS))


def forward_kernel(bad_ref, q_ref, kl_ref, kc_ref, kr_ref, _, o_ref, lse_ref):
    bads = (bad_ref[0], jnp.float32(0.0), bad_ref[1])
    sides = (kl_ref, kc_ref, kr_ref)
    for b in range(ROWS):
        query = q_ref[b, 0, 0]
        scores = []
        for side in range(3):
            for u in near_rows(b):
                scores.append((side, u, dot(sides[side][u, 0, 0], query, NT)))
        top = None
        for side in range(3):
            local = None
            for at, _, s in scores:
                if at == side:
                    one = jnp.max(s, axis=0, keepdims=True)
                    local = one if local is None else jnp.maximum(local, one)
            local = local - bads[side]
            top = local if top is None else jnp.maximum(top, local)
        top = top * BASE2
        total = None
        mixed = None
        for side, u, s in scores:
            p = jnp.exp2(s * BASE2 - (top + bads[side]))
            one = jnp.sum(p, axis=0, keepdims=True)
            total = one if total is None else total + one
            term = dot(sides[side][u, 0, 1], p.astype(jnp.bfloat16), TN)
            mixed = term if mixed is None else mixed + term
        mixed = mixed * (1.0 / total)
        o_ref[b, 0, 0] = mixed.T.astype(jnp.bfloat16)
        lse_ref[0, b] = top + jnp.log2(total)


def column_spec(count, tokens):
    return pl.BlockSpec((ROWS, 1, count, tokens, HEAD_DIM), lambda h: (0, h, 0, 0, 0))


def attend_forward(bad, q, kv_left, kv, kv_right, after):
    tokens = q.shape[3]
    group = q.shape[1]
    return pl.pallas_call(
        forward_kernel,
        grid=(group,),
        in_specs=[pl.BlockSpec(memory_space=pltpu.SMEM), column_spec(1, tokens)]
        + [column_spec(2, tokens)] * 3
        + [pl.BlockSpec(memory_space=pl.ANY)],
        out_specs=[
            column_spec(1, tokens),
            pl.BlockSpec((1, ROWS, 1, tokens), lambda h: (h, 0, 0, 0)),
        ],
        out_shape=[
            jax.ShapeDtypeStruct(q.shape, jnp.bfloat16),
            jax.ShapeDtypeStruct((group, ROWS, 1, tokens), jnp.float32),
        ],
        cost_estimate=cost(100),
        compiler_params=params(),
    )(bad, q, kv_left, kv, kv_right, after)


def backward_kernel(
    bad_ref,
    q_ref,
    kl_ref,
    kc_ref,
    kr_ref,
    do_ref,
    o_ref,
    lse_ref,
    *rest,
):
    dq_ref, dl_ref, dc_ref, dr_ref, dqt_ref, row_ref = rest[-6:]
    bads = (bad_ref[0], jnp.float32(0.0), bad_ref[1])
    sides = (kl_ref, kc_ref, kr_ref)
    outs = (dl_ref, dc_ref, dr_ref)
    for b in range(ROWS):
        product = do_ref[b, 0, 0].astype(jnp.float32) * o_ref[b, 0, 0].astype(jnp.float32)
        row_ref[b] = jnp.sum(product.T, axis=0, keepdims=True)
    seen = set()
    for side in (0, 2, 1):
        for u in range(ROWS):
            key = sides[side][u, 0, 0]
            value = sides[side][u, 0, 1]
            dk = None
            dv = None
            for b in near_rows(u):
                query = q_ref[b, 0, 0]
                grad = do_ref[b, 0, 0]
                s = dot(key, query, NT)
                p = jnp.exp2(s * BASE2 - (lse_ref[0, b] + bads[side]))
                e = dot(value, grad, NT)
                g = (p * (e - row_ref[b])).astype(jnp.bfloat16)
                tv = dot(p.astype(jnp.bfloat16), grad, NN)
                tk = dot(g, query, NN)
                tq = dot(key, g, TN)
                dv = tv if dv is None else dv + tv
                dk = tk if dk is None else dk + tk
                if b in seen:
                    dqt_ref[b] += tq
                else:
                    seen.add(b)
                    dqt_ref[b] = tq
            outs[side][u, 0, 0] = (dk * SCALE).astype(outs[side].dtype)
            outs[side][u, 0, 1] = dv.astype(outs[side].dtype)
    for b in range(ROWS):
        dq_ref[b, 0, 0] = (dqt_ref[b] * SCALE).T.astype(jnp.bfloat16)


def heads_spec(first, count, tokens):
    return pl.BlockSpec((ROWS, 1, count, tokens, HEAD_DIM), lambda i: (0, first + i, 0, 0, 0))


def attend_backward(first, heads, bad, q, kv_left, kv, kv_right, grad, mixed, lse, after):
    tokens = q.shape[3]
    return pl.pallas_call(
        backward_kernel,
        grid=(heads,),
        in_specs=[pl.BlockSpec(memory_space=pltpu.SMEM), heads_spec(first, 1, tokens)]
        + [heads_spec(first, 2, tokens)] * 3
        + [heads_spec(first, 1, tokens)] * 2
        + [pl.BlockSpec((1, ROWS, 1, tokens), lambda i: (first + i, 0, 0, 0))]
        + [pl.BlockSpec(memory_space=pl.ANY)] * len(after),
        out_specs=[heads_spec(0, 1, tokens)] + [heads_spec(0, 2, tokens)] * 3,
        out_shape=[bf16(ROWS, heads, 1, tokens, HEAD_DIM)]
        + [bf16(ROWS, heads, 2, tokens, HEAD_DIM)] * 3,
        scratch_shapes=[
            pltpu.VMEM((ROWS, HEAD_DIM, tokens), jnp.float32),
            pltpu.VMEM((ROWS, 1, tokens), jnp.float32),
        ],
        cost_estimate=cost(100),
        compiler_params=params(),
    )(bad, q, kv_left, kv, kv_right, grad, mixed, lse, *after)


def total_kernel(dq_ref, own_ref, a_ref, b_ref, _, out_ref):
    for h in range(out_ref.shape[1]):
        for r in range(ROWS):
            out_ref[r, h, 0] = dq_ref[r, h, 0]
            for t in range(2):
                total = own_ref[r, h, t].astype(jnp.float32) + a_ref[r, h, t].astype(jnp.float32)
                total = total + b_ref[r, h, t].astype(jnp.float32)
                out_ref[r, h, 1 + t] = total.astype(jnp.bfloat16)


def totals(dq, own, a, b, after):
    heads, tokens = dq.shape[1], dq.shape[3]
    vmem = pl.BlockSpec(memory_space=pltpu.VMEM)
    return pl.pallas_call(
        total_kernel,
        in_specs=[vmem] * 4 + [pl.BlockSpec(memory_space=pl.ANY)],
        out_specs=vmem,
        out_shape=bf16(ROWS, heads, 3, tokens, HEAD_DIM),
        cost_estimate=cost(0.1),
        compiler_params=params(),
    )(dq, own, a, b, after)


def lane_sums(products):
    rows = products[0].shape[0]
    product = jnp.concatenate(products, axis=0)
    high = product.astype(jnp.bfloat16)
    low = (product - high.astype(jnp.float32)).astype(jnp.bfloat16)
    ones = jnp.ones((2 * HEAD_DIM, HEAD_DIM), jnp.bfloat16)
    sums = dot(jnp.concatenate([high, low], axis=1), ones, NN)
    return [sums[i * rows : (i + 1) * rows] for i in range(len(products))]


def temporal_weights(probes, anchors):
    scores = lane_sums([p * a for p in probes for a in anchors])
    weights = []
    for f in range(PARTS):
        row = [s * SCALE for s in scores[f * PARTS : (f + 1) * PARTS]]
        top = functools.reduce(jnp.maximum, row)
        shifted = [jnp.exp(s - top) for s in row]
        inverse = 1.0 / functools.reduce(jnp.add, shifted)
        weights.append([s * inverse for s in shifted])
    return weights


def rounded(x):
    return x.astype(jnp.bfloat16).astype(jnp.float32)


def temporal_forward_kernel(*refs):
    ins, outs = refs[:PARTS], refs[PARTS:]
    parts = [[ref[0, t].astype(jnp.float32) for ref in ins] for t in range(3)]
    weights = temporal_weights(parts[0], parts[1])
    for g in range(PARTS):
        terms = [rounded(weights[f][g]) * parts[2][f] for f in range(PARTS)]
        outs[g][0, 0] = functools.reduce(jnp.add, terms).astype(jnp.bfloat16)


def temporal_backward_kernel(*refs):
    ins, mixed_refs, outs = refs[:PARTS], refs[PARTS : 2 * PARTS], refs[-PARTS:]
    parts = [[ref[0, t].astype(jnp.float32) for ref in ins] for t in range(3)]
    mixed = [ref[0, 0].astype(jnp.float32) for ref in mixed_refs]
    weights = temporal_weights(parts[0], parts[1])
    sums = lane_sums([u * m for u in parts[2] for m in mixed])
    anchor_grads = [None] * PARTS
    for f in range(PARTS):
        grads = sums[f * PARTS : (f + 1) * PARTS]
        row = functools.reduce(jnp.add, [w * c for w, c in zip(weights[f], grads)])
        scores = [rounded(w * (c - row)) for w, c in zip(weights[f], grads)]
        probe = functools.reduce(jnp.add, [s * parts[1][g] for g, s in enumerate(scores)])
        outs[f][0, 0] = (probe * SCALE).astype(jnp.bfloat16)
        for g in range(PARTS):
            term = scores[g] * parts[0][f]
            anchor_grads[g] = term if f == 0 else anchor_grads[g] + term
    for g in range(PARTS):
        outs[g][0, 1] = (anchor_grads[g] * SCALE).astype(jnp.bfloat16)


def temporal_call(kernel, arrays, count_out, told, after=()):
    group, _, tokens, _ = arrays[0].shape
    rows = 128

    def spec(count):
        return pl.BlockSpec((1, count, rows, HEAD_DIM), lambda h, i: (h, 0, i, 0))

    return pl.pallas_call(
        kernel,
        grid=(group, tokens // rows),
        in_specs=[spec(a.shape[1]) for a in arrays]
        + [pl.BlockSpec(memory_space=pl.ANY)] * len(after),
        out_specs=[spec(count_out)] * PARTS,
        out_shape=[bf16(group, count_out, tokens, HEAD_DIM)] * PARTS,
        cost_estimate=cost(told),
        compiler_params=params(),
    )(*arrays, *after)


def swap(x, axis):
    return lax.all_to_all(x, axis, split_axis=0, concat_axis=0, tiled=True)


def shift_right(x):
    count = lax.axis_size("wa")
    return lax.ppermute(x, "wa", [(i, i + 1) for i in range(count - 1)])


def shift_left(x):
    count = lax.axis_size("wa")
    return lax.ppermute(x, "wa", [(i + 1, i) for i in range(count - 1)])


def shards(queries, tile_keys, values, probes, anchors, upstream):
    shape = queries.shape
    tokens = shape[2] * shape[3]

    def flat(x):
        return x.reshape(tokens, shape[-1])

    place = lax.axis_index("wa")
    bad = jnp.stack([place == 0, place == lax.axis_size("wa") - 1]).astype(jnp.float32) * BIG

    kv_sent = pack([flat(tile_keys), flat(values)])
    kv = swap(kv_sent, "ha")
    pau = trade(pack_partners([flat(probes), flat(anchors), flat(upstream)], [kv_sent]))
    kv_left = shift_right(kv)
    kv_right = shift_left(kv)
    forward_sent = temporal_call(temporal_forward_kernel, pau, 1, 100)
    q = swap(pack([flat(queries)], forward_sent[:1]), "ha")
    grad_sent = join_partners(trade(forward_sent))
    grad = swap(grad_sent, "ha")
    mixed, lse = attend_forward(bad, q, kv_left, kv, kv_right, grad_sent)
    mixed_sent = split_partners(swap(mixed, "ha"))
    mixed_parts = trade(mixed_sent)
    def backward(first, heads, after):
        dq, to_left, own, to_right = attend_backward(
            first, heads, bad, q, kv_left, kv, kv_right, grad, mixed, lse, after
        )
        return dq, own, shift_right(to_right), shift_left(to_left)

    early = GROUP - 1
    one = backward(0, early, [])
    two = backward(early, 1, [mixed_sent[0], one[0]])
    summed = [totals(*one, two[0])]
    times_sent = temporal_call(
        temporal_backward_kernel, pau + mixed_parts, 2, 100, summed
    )
    summed = [swap(summed[0], "ha")]
    summed.append(swap(totals(*two, summed[0]), "ha"))
    probe_grad, anchor_grad = unpack_partners(trade(times_sent), [])
    query_grad, key_grad, value_grad = unpack_heads(summed)
    outs = (query_grad, key_grad, value_grad, probe_grad, anchor_grad)
    return tuple(x.reshape(shape) for x in outs)


def solution(mesh):
    spec = P(None, "tm", "ha", "wa", None)
    return jax.shard_map(
        shards,
        mesh=mesh,
        in_specs=(spec,) * 6,
        out_specs=(spec,) * 5,
        check_vma=False,
    )
```

```python
import functools

import jax
import jax.numpy as jnp
from jax import lax
from jax.experimental import pallas as pl
from jax.experimental.pallas import tpu as pltpu
from jax.sharding import PartitionSpec as P

HEADS = 12
HEAD_DIM = 128
PARTS = 4
GROUP = HEADS // PARTS
ROWS = 4
BIG = 1e30
SCALE = HEAD_DIM ** (-0.5)
LOG2E = 1.4426950408889634
BASE2 = SCALE * LOG2E

NT = (((1,), (1,)), ((), ()))
NN = (((1,), (0,)), ((), ()))
TN = (((0,), (0,)), ((), ()))


def dot(a, b, dims):
    return lax.dot_general(a, b, dims, preferred_element_type=jnp.float32)


def params():
    return pltpu.CompilerParams(vmem_limit_bytes=63 * 1024 * 1024)


def cost(microseconds):
    return pl.CostEstimate(
        flops=int(microseconds * 1e9), bytes_accessed=1024, transcendentals=0
    )


def move(inputs, out_shapes, plan, axis=None, after=(), told=0.1):
    first = len(inputs) + len(after)

    def kernel(*refs):
        ins = refs[: len(inputs)]
        outs = refs[first:]
        me = 0 if axis is None else lax.axis_index(axis)
        for i, at, o, to in plan(me):
            outs[o][to] = ins[i][at]

    return pl.pallas_call(
        kernel,
        in_specs=[pl.BlockSpec(memory_space=pltpu.VMEM)] * len(inputs)
        + [pl.BlockSpec(memory_space=pl.ANY)] * len(after),
        out_specs=[pl.BlockSpec(memory_space=pltpu.VMEM)] * len(out_shapes),
        out_shape=out_shapes,
        cost_estimate=cost(told),
        compiler_params=params(),
    )(*inputs, *after)


def columns(group, head):
    start = (group * GROUP + head) * HEAD_DIM
    if not isinstance(start, int):
        start = pl.multiple_of(start, HEAD_DIM)
    return (slice(None), pl.ds(start, HEAD_DIM))


def bf16(*shape):
    return jax.ShapeDtypeStruct(shape, jnp.bfloat16)


def pack(arrays, after=(), told=0.1):
    tokens = arrays[0].shape[0]
    cells = [(a, d, h) for d in range(PARTS) for h in range(GROUP) for a in range(len(arrays))]
    return move(
        arrays,
        [bf16(PARTS, GROUP, len(arrays), tokens, HEAD_DIM)],
        lambda me: [(a, columns(d, h), 0, (d, h, a)) for a, d, h in cells],
        after=after,
        told=told,
    )[0]


def pack_partners(arrays, after=()):
    tokens = arrays[0].shape[0]
    cells = [(a, s, h) for s in range(PARTS) for h in range(GROUP) for a in range(len(arrays))]
    return move(
        arrays,
        [bf16(GROUP, len(arrays), tokens, HEAD_DIM)] * PARTS,
        lambda me: [(a, columns(me ^ s, h), s, (h, a)) for a, s, h in cells],
        "tm",
        after,
    )


def unpack_partners(chunks, after):
    _, count, tokens, _ = chunks[0].shape
    cells = [(a, s, h) for s in range(PARTS) for h in range(GROUP) for a in range(count)]
    return move(
        chunks,
        [bf16(tokens, HEADS * HEAD_DIM)] * count,
        lambda me: [(s, (h, a), a, columns(me ^ s, h)) for a, s, h in cells],
        "tm",
        after,
        told=100,
    )


def join_partners(chunks):
    return move(
        chunks,
        [bf16(PARTS, *chunks[0].shape)],
        lambda me: [(s, (slice(None),), 0, (me ^ s,)) for s in range(PARTS)],
        "tm",
    )[0]


def split_partners(block):
    return move(
        [block],
        [bf16(*block.shape[1:])] * PARTS,
        lambda me: [(0, (me ^ s,), s, (slice(None),)) for s in range(PARTS)],
        "tm",
    )


def unpack_heads(blocks):
    count, tokens = blocks[0].shape[2:4]
    heads = [(n, i) for n, block in enumerate(blocks) for i in range(block.shape[1])]
    cells = [(a, d, h) for h in range(GROUP) for d in range(PARTS) for a in range(count)]
    return move(
        blocks,
        [bf16(tokens, HEADS * HEAD_DIM)] * count,
        lambda me: [
            (heads[h][0], (d, heads[h][1], a), a, columns(d, h)) for a, d, h in cells
        ],
    )


def trade(chunks):
    out = [chunks[0]]
    for s in range(1, PARTS):
        out.append(lax.ppermute(chunks[s], "tm", [(i, i ^ s) for i in range(PARTS)]))
    return out


def near_rows(row):
    return max(row - 1, 0), min(row + 2, ROWS)


def tiles(ref, rows, tensor):
    low, high = rows
    block = ref[low:high, 0, tensor]
    return block.reshape((high - low) * block.shape[1], HEAD_DIM)


def forward_kernel(bad_ref, q_ref, other_ref, own_ref, partner_ref, _, o_ref, lse_ref, vt_ref):
    bad = bad_ref[0]
    sides = (other_ref, own_ref, partner_ref)
    tokens = q_ref.shape[3]
    for side in range(3):
        vt_ref[side] = tiles(sides[side], (0, ROWS), 1).T
    for b in range(ROWS):
        query = q_ref[b, 0, 0]
        rows = near_rows(b)
        span = slice(rows[0] * tokens, rows[1] * tokens)
        scores = [dot(tiles(ref, rows, 0), query, NT) for ref in sides]
        tops = [jnp.max(s, axis=0, keepdims=True) for s in scores]
        top = functools.reduce(jnp.maximum, [tops[0] - bad] + tops[1:]) * BASE2
        total = None
        mixed = None
        for side, s in enumerate(scores):
            p = jnp.exp2(s * BASE2 - (top + bad if side == 0 else top))
            one = jnp.sum(p, axis=0, keepdims=True)
            total = one if total is None else total + one
            term = dot(vt_ref[side, :, span], p.astype(jnp.bfloat16), NN)
            mixed = term if mixed is None else mixed + term
        mixed = mixed * (1.0 / total)
        o_ref[b, 0, 0] = mixed.T.astype(jnp.bfloat16)
        lse_ref[0, :, b * tokens : (b + 1) * tokens] = top + jnp.log2(total)


def column_spec(count, tokens):
    return pl.BlockSpec((ROWS, 1, count, tokens, HEAD_DIM), lambda h: (0, h, 0, 0, 0))


def attend_forward(bad, q, kv_other, kv, kv_partner, after):
    tokens = q.shape[3]
    group = q.shape[1]
    return pl.pallas_call(
        forward_kernel,
        grid=(group,),
        in_specs=[pl.BlockSpec(memory_space=pltpu.SMEM), column_spec(1, tokens)]
        + [column_spec(2, tokens)] * 3
        + [pl.BlockSpec(memory_space=pl.ANY)],
        out_specs=[
            column_spec(1, tokens),
            pl.BlockSpec((1, 1, ROWS * tokens), lambda h: (h, 0, 0)),
        ],
        out_shape=[
            jax.ShapeDtypeStruct(q.shape, jnp.bfloat16),
            jax.ShapeDtypeStruct((group, 1, ROWS * tokens), jnp.float32),
        ],
        scratch_shapes=[pltpu.VMEM((3, HEAD_DIM, ROWS * tokens), jnp.bfloat16)],
        cost_estimate=cost(100),
        compiler_params=params(),
    )(bad, q, kv_other, kv, kv_partner, after)


def backward_kernel(
    bad_ref, q_ref, other_ref, own_ref, partner_ref, do_ref, o_ref, lse_ref, *rest
):
    dq_ref, d_other_ref, d_own_ref, d_partner_ref, dqt_ref, row_ref = rest[-6:]
    bad = bad_ref[0]
    sides = (other_ref, own_ref, partner_ref)
    outs = (d_other_ref, d_own_ref, d_partner_ref)
    tokens = q_ref.shape[3]
    for b in range(ROWS):
        product = do_ref[b, 0, 0].astype(jnp.float32) * o_ref[b, 0, 0].astype(jnp.float32)
        row_ref[:, b * tokens : (b + 1) * tokens] = jnp.sum(product.T, axis=0, keepdims=True)
    dqt_ref[...] = jnp.zeros_like(dqt_ref)
    for side in range(3):
        for u in range(ROWS):
            rows = near_rows(u)
            span = slice(rows[0] * tokens, rows[1] * tokens)
            key = sides[side][u, 0, 0]
            query = tiles(q_ref, rows, 0)
            grad = tiles(do_ref, rows, 0)
            lse = lse_ref[0, :, span]
            if side == 0:
                lse = lse + bad
            p = jnp.exp2(dot(key, query, NT) * BASE2 - lse)
            e = dot(sides[side][u, 0, 1], grad, NT)
            g = (p * (e - row_ref[:, span])).astype(jnp.bfloat16)
            dk = dot(g, query, NN) * SCALE
            dv = dot(p.astype(jnp.bfloat16), grad, NN)
            dqt_ref[:, span] += dot(key, g, TN)
            outs[side][u, 0, 0] = dk.astype(outs[side].dtype)
            outs[side][u, 0, 1] = dv.astype(outs[side].dtype)
    for b in range(ROWS):
        dq = dqt_ref[:, b * tokens : (b + 1) * tokens] * SCALE
        dq_ref[b, 0, 0] = dq.T.astype(jnp.bfloat16)


def heads_spec(first, count, tokens):
    return pl.BlockSpec((ROWS, 1, count, tokens, HEAD_DIM), lambda i: (0, first + i, 0, 0, 0))


def attend_backward(first, heads, bad, q, kv_other, kv, kv_partner, grad, mixed, lse, after):
    tokens = q.shape[3]
    return pl.pallas_call(
        backward_kernel,
        grid=(heads,),
        in_specs=[pl.BlockSpec(memory_space=pltpu.SMEM), heads_spec(first, 1, tokens)]
        + [heads_spec(first, 2, tokens)] * 3
        + [heads_spec(first, 1, tokens)] * 2
        + [pl.BlockSpec((1, 1, ROWS * tokens), lambda i: (first + i, 0, 0))]
        + [pl.BlockSpec(memory_space=pl.ANY)] * len(after),
        out_specs=[heads_spec(0, 1, tokens)] + [heads_spec(0, 2, tokens)] * 3,
        out_shape=[bf16(ROWS, heads, 1, tokens, HEAD_DIM)]
        + [bf16(ROWS, heads, 2, tokens, HEAD_DIM)] * 3,
        scratch_shapes=[
            pltpu.VMEM((HEAD_DIM, ROWS * tokens), jnp.float32),
            pltpu.VMEM((1, ROWS * tokens), jnp.float32),
        ],
        cost_estimate=cost(100),
        compiler_params=params(),
    )(bad, q, kv_other, kv, kv_partner, grad, mixed, lse, *after)


def total_kernel(dq_ref, own_ref, a_ref, b_ref, _, out_ref):
    for h in range(out_ref.shape[1]):
        for r in range(ROWS):
            out_ref[r, h, 0] = dq_ref[r, h, 0]
            for t in range(2):
                total = own_ref[r, h, t].astype(jnp.float32) + a_ref[r, h, t].astype(jnp.float32)
                total = total + b_ref[r, h, t].astype(jnp.float32)
                out_ref[r, h, 1 + t] = total.astype(jnp.bfloat16)


def totals(dq, own, a, b, after):
    heads, tokens = dq.shape[1], dq.shape[3]
    vmem = pl.BlockSpec(memory_space=pltpu.VMEM)
    return pl.pallas_call(
        total_kernel,
        in_specs=[vmem] * 4 + [pl.BlockSpec(memory_space=pl.ANY)],
        out_specs=vmem,
        out_shape=bf16(ROWS, heads, 3, tokens, HEAD_DIM),
        cost_estimate=cost(0.1),
        compiler_params=params(),
    )(dq, own, a, b, after)


def lane_sums(products):
    rows = products[0].shape[0]
    product = jnp.concatenate(products, axis=0)
    high = product.astype(jnp.bfloat16)
    low = (product - high.astype(jnp.float32)).astype(jnp.bfloat16)
    ones = jnp.ones((2 * HEAD_DIM, HEAD_DIM), jnp.bfloat16)
    sums = dot(jnp.concatenate([high, low], axis=1), ones, NN)
    return [sums[i * rows : (i + 1) * rows] for i in range(len(products))]


def temporal_weights(probes, anchors):
    scores = lane_sums([p * a for p in probes for a in anchors])
    weights = []
    for f in range(PARTS):
        row = [s * SCALE for s in scores[f * PARTS : (f + 1) * PARTS]]
        top = functools.reduce(jnp.maximum, row)
        shifted = [jnp.exp(s - top) for s in row]
        inverse = 1.0 / functools.reduce(jnp.add, shifted)
        weights.append([s * inverse for s in shifted])
    return weights


def rounded(x):
    return x.astype(jnp.bfloat16).astype(jnp.float32)


def temporal_forward_kernel(*refs):
    ins, outs = refs[:PARTS], refs[-PARTS:]
    parts = [[ref[0, t].astype(jnp.float32) for ref in ins] for t in range(3)]
    weights = temporal_weights(parts[0], parts[1])
    for g in range(PARTS):
        terms = [rounded(weights[f][g]) * parts[2][f] for f in range(PARTS)]
        outs[g][0, 0] = functools.reduce(jnp.add, terms).astype(jnp.bfloat16)


def temporal_backward_kernel(*refs):
    ins, mixed_refs, outs = refs[:PARTS], refs[PARTS : 2 * PARTS], refs[-PARTS:]
    parts = [[ref[0, t].astype(jnp.float32) for ref in ins] for t in range(3)]
    mixed = [ref[0, 0].astype(jnp.float32) for ref in mixed_refs]
    weights = temporal_weights(parts[0], parts[1])
    sums = lane_sums([u * m for u in parts[2] for m in mixed])
    anchor_grads = [None] * PARTS
    for f in range(PARTS):
        grads = sums[f * PARTS : (f + 1) * PARTS]
        row = functools.reduce(jnp.add, [w * c for w, c in zip(weights[f], grads)])
        scores = [rounded(w * (c - row)) for w, c in zip(weights[f], grads)]
        probe = functools.reduce(jnp.add, [s * parts[1][g] for g, s in enumerate(scores)])
        outs[f][0, 0] = (probe * SCALE).astype(jnp.bfloat16)
        for g in range(PARTS):
            term = scores[g] * parts[0][f]
            anchor_grads[g] = term if f == 0 else anchor_grads[g] + term
    for g in range(PARTS):
        outs[g][0, 1] = (anchor_grads[g] * SCALE).astype(jnp.bfloat16)


def temporal_call(kernel, arrays, count_out, told, after=()):
    group, _, tokens, _ = arrays[0].shape
    rows = 128

    def spec(count):
        return pl.BlockSpec((1, count, rows, HEAD_DIM), lambda h, i: (h, 0, i, 0))

    return pl.pallas_call(
        kernel,
        grid=(group, tokens // rows),
        in_specs=[spec(a.shape[1]) for a in arrays]
        + [pl.BlockSpec(memory_space=pl.ANY)] * len(after),
        out_specs=[spec(count_out)] * PARTS,
        out_shape=[bf16(group, count_out, tokens, HEAD_DIM)] * PARTS,
        cost_estimate=cost(told),
        compiler_params=params(),
    )(*arrays, *after)


def swap(x, axis):
    return lax.all_to_all(x, axis, split_axis=0, concat_axis=0, tiled=True)


def trade_partner(x):
    return lax.ppermute(x, "wa", [(i, i ^ 1) for i in range(lax.axis_size("wa"))])


def trade_other(x):
    firsts = range(1, lax.axis_size("wa") - 1, 2)
    pairs = [(i, i + 1) for i in firsts] + [(i + 1, i) for i in firsts]
    return lax.ppermute(x, "wa", pairs)


def shards(queries, tile_keys, values, probes, anchors, upstream):
    shape = queries.shape
    tokens = shape[2] * shape[3]

    def flat(x):
        return x.reshape(tokens, shape[-1])

    place = lax.axis_index("wa")
    no_other = (place == 0) | (place == lax.axis_size("wa") - 1)
    bad = no_other.astype(jnp.float32).reshape(1) * BIG

    kv_sent = pack([flat(tile_keys), flat(values)])
    kv = swap(kv_sent, "ha")
    kv_other = trade_other(kv)
    kv_partner = trade_partner(kv)
    pau_sent = pack_partners([flat(probes), flat(anchors), flat(upstream)], [kv_sent])
    pau = trade(pau_sent)
    q_sent = pack([flat(queries)], pau_sent[:1])
    q = swap(q_sent, "ha")
    grad_parts = trade(temporal_call(temporal_forward_kernel, pau, 1, 100, [kv, q_sent]))
    grad_sent = join_partners(grad_parts)
    grad = swap(grad_sent, "ha")
    mixed, lse = attend_forward(bad, q, kv_other, kv, kv_partner, grad_sent)
    mixed_sent = split_partners(swap(mixed, "ha"))
    mixed_parts = trade(mixed_sent)
    def backward(first, heads, after):
        dq, to_other, own, to_partner = attend_backward(
            first, heads, bad, q, kv_other, kv, kv_partner, grad, mixed, lse, after
        )
        return dq, own, trade_other(to_other), trade_partner(to_partner)

    early = GROUP - 1
    one = backward(0, early, [])
    two = backward(early, 1, [mixed_sent[0], one[0]])
    summed = [totals(*one, two[0])]
    times_sent = temporal_call(
        temporal_backward_kernel, pau + mixed_parts, 2, 100, summed
    )
    summed = [swap(summed[0], "ha")]
    summed.append(swap(totals(*two, summed[0]), "ha"))
    probe_grad, anchor_grad = unpack_partners(trade(times_sent), [])
    query_grad, key_grad, value_grad = unpack_heads(summed)
    outs = (query_grad, key_grad, value_grad, probe_grad, anchor_grad)
    return tuple(x.reshape(shape) for x in outs)


def solution(mesh):
    spec = P(None, "tm", "ha", "wa", None)
    return jax.shard_map(
        shards,
        mesh=mesh,
        in_specs=(spec,) * 6,
        out_specs=(spec,) * 5,
        check_vma=False,
    )
```

```python
import functools

import jax
import jax.numpy as jnp
from jax import lax
from jax.experimental import pallas as pl
from jax.experimental.pallas import tpu as pltpu
from jax.sharding import PartitionSpec as P

HEADS = 12
HEAD_DIM = 128
PARTS = 4
GROUP = HEADS // PARTS
ROWS = 4
BIG = 1e30
SCALE = HEAD_DIM ** (-0.5)
LOG2E = 1.4426950408889634
BASE2 = SCALE * LOG2E

NT = (((1,), (1,)), ((), ()))
NN = (((1,), (0,)), ((), ()))
TN = (((0,), (0,)), ((), ()))


def dot(a, b, dims):
    return lax.dot_general(a, b, dims, preferred_element_type=jnp.float32)


def params():
    return pltpu.CompilerParams(vmem_limit_bytes=63 * 1024 * 1024)


def cost(microseconds):
    return pl.CostEstimate(
        flops=int(microseconds * 1e9), bytes_accessed=1024, transcendentals=0
    )


def move(inputs, out_shapes, plan, axis=None, after=(), told=0.1):
    first = len(inputs) + len(after)

    def kernel(*refs):
        ins = refs[: len(inputs)]
        outs = refs[first:]
        me = 0 if axis is None else lax.axis_index(axis)
        for i, at, o, to in plan(me):
            outs[o][to] = ins[i][at]

    return pl.pallas_call(
        kernel,
        in_specs=[pl.BlockSpec(memory_space=pltpu.VMEM)] * len(inputs)
        + [pl.BlockSpec(memory_space=pl.ANY)] * len(after),
        out_specs=[pl.BlockSpec(memory_space=pltpu.VMEM)] * len(out_shapes),
        out_shape=out_shapes,
        cost_estimate=cost(told),
        compiler_params=params(),
    )(*inputs, *after)


def columns(group, head):
    start = (group * GROUP + head) * HEAD_DIM
    if not isinstance(start, int):
        start = pl.multiple_of(start, HEAD_DIM)
    return (slice(None), pl.ds(start, HEAD_DIM))


def bf16(*shape):
    return jax.ShapeDtypeStruct(shape, jnp.bfloat16)


def pack(arrays, after=(), told=0.1):
    tokens = arrays[0].shape[0]
    cells = [(a, d, h) for d in range(PARTS) for h in range(GROUP) for a in range(len(arrays))]
    return move(
        arrays,
        [bf16(PARTS, GROUP, len(arrays), tokens, HEAD_DIM)],
        lambda me: [(a, columns(d, h), 0, (d, h, a)) for a, d, h in cells],
        after=after,
        told=told,
    )[0]


def pack_partners(arrays, after=()):
    tokens = arrays[0].shape[0]
    cells = [(a, s, h) for s in range(PARTS) for h in range(GROUP) for a in range(len(arrays))]
    return move(
        arrays,
        [bf16(GROUP, len(arrays), tokens, HEAD_DIM)] * PARTS,
        lambda me: [(a, columns(me ^ s, h), s, (h, a)) for a, s, h in cells],
        "tm",
        after,
    )


def unpack_partners(chunks, after):
    _, count, tokens, _ = chunks[0].shape
    cells = [(a, s, h) for s in range(PARTS) for h in range(GROUP) for a in range(count)]
    return move(
        chunks,
        [bf16(tokens, HEADS * HEAD_DIM)] * count,
        lambda me: [(s, (h, a), a, columns(me ^ s, h)) for a, s, h in cells],
        "tm",
        after,
        told=100,
    )


def join_partners(chunks):
    return move(
        chunks,
        [bf16(PARTS, *chunks[0].shape)],
        lambda me: [(s, (slice(None),), 0, (me ^ s,)) for s in range(PARTS)],
        "tm",
    )[0]


def split_partners(block):
    return move(
        [block],
        [bf16(*block.shape[1:])] * PARTS,
        lambda me: [(0, (me ^ s,), s, (slice(None),)) for s in range(PARTS)],
        "tm",
    )


def unpack_heads(early, late):
    tokens = early.shape[2]
    places = [[(0, 0), (0, 1), (0, 2)]]
    for h in range(GROUP - 1):
        places.append([(0, 3 + h), (1, 2 * h), (1, 2 * h + 1)])
    cells = [(a, d, h) for h in range(GROUP) for d in range(PARTS) for a in range(3)]
    return move(
        [early, late],
        [bf16(tokens, HEADS * HEAD_DIM)] * 3,
        lambda me: [
            (places[h][a][0], (d, places[h][a][1]), a, columns(d, h)) for a, d, h in cells
        ],
    )


def trade(chunks):
    out = [chunks[0]]
    for s in range(1, PARTS):
        out.append(lax.ppermute(chunks[s], "tm", [(i, i ^ s) for i in range(PARTS)]))
    return out


def near_rows(row):
    return max(row - 1, 0), min(row + 2, ROWS)


def tiles(ref, rows, tensor):
    low, high = rows
    block = ref[low:high, 0, tensor]
    return block.reshape((high - low) * block.shape[1], HEAD_DIM)


def forward_kernel(bad_ref, q_ref, other_ref, own_ref, partner_ref, _, o_ref, lse_ref, vt_ref):
    bad = bad_ref[0]
    sides = (other_ref, own_ref, partner_ref)
    tokens = q_ref.shape[3]
    for side in range(3):
        vt_ref[side] = tiles(sides[side], (0, ROWS), 1).T
    for b in range(ROWS):
        query = q_ref[b, 0, 0]
        rows = near_rows(b)
        span = slice(rows[0] * tokens, rows[1] * tokens)
        scores = [dot(tiles(ref, rows, 0), query, NT) for ref in sides]
        tops = [jnp.max(s, axis=0, keepdims=True) for s in scores]
        top = functools.reduce(jnp.maximum, [tops[0] - bad] + tops[1:]) * BASE2
        total = None
        mixed = None
        for side, s in enumerate(scores):
            p = jnp.exp2(s * BASE2 - (top + bad if side == 0 else top))
            one = jnp.sum(p, axis=0, keepdims=True)
            total = one if total is None else total + one
            term = dot(vt_ref[side, :, span], p.astype(jnp.bfloat16), NN)
            mixed = term if mixed is None else mixed + term
        mixed = mixed * (1.0 / total)
        o_ref[b, 0, 0] = mixed.T.astype(jnp.bfloat16)
        lse_ref[0, :, b * tokens : (b + 1) * tokens] = top + jnp.log2(total)


def column_spec(count, tokens):
    return pl.BlockSpec((ROWS, 1, count, tokens, HEAD_DIM), lambda h: (0, h, 0, 0, 0))


def attend_forward(bad, q, kv_other, kv, kv_partner, after):
    tokens = q.shape[3]
    group = q.shape[1]
    return pl.pallas_call(
        forward_kernel,
        grid=(group,),
        in_specs=[pl.BlockSpec(memory_space=pltpu.SMEM), column_spec(1, tokens)]
        + [column_spec(2, tokens)] * 3
        + [pl.BlockSpec(memory_space=pl.ANY)],
        out_specs=[
            column_spec(1, tokens),
            pl.BlockSpec((1, 1, ROWS * tokens), lambda h: (h, 0, 0)),
        ],
        out_shape=[
            jax.ShapeDtypeStruct(q.shape, jnp.bfloat16),
            jax.ShapeDtypeStruct((group, 1, ROWS * tokens), jnp.float32),
        ],
        scratch_shapes=[pltpu.VMEM((3, HEAD_DIM, ROWS * tokens), jnp.bfloat16)],
        cost_estimate=cost(100),
        compiler_params=params(),
    )(bad, q, kv_other, kv, kv_partner, after)


def backward_kernel(
    bad_ref, q_ref, other_ref, own_ref, partner_ref, do_ref, o_ref, lse_ref, *rest
):
    dq_ref, d_other_ref, d_own_ref, d_partner_ref, dqt_ref, row_ref = rest[-6:]
    bad = bad_ref[0]
    sides = (other_ref, own_ref, partner_ref)
    outs = (d_other_ref, d_own_ref, d_partner_ref)
    tokens = q_ref.shape[3]
    for b in range(ROWS):
        product = do_ref[b, 0, 0].astype(jnp.float32) * o_ref[b, 0, 0].astype(jnp.float32)
        row_ref[:, b * tokens : (b + 1) * tokens] = jnp.sum(product.T, axis=0, keepdims=True)
    dqt_ref[...] = jnp.zeros_like(dqt_ref)
    for side in range(3):
        for u in range(ROWS):
            rows = near_rows(u)
            span = slice(rows[0] * tokens, rows[1] * tokens)
            key = sides[side][u, 0, 0]
            query = tiles(q_ref, rows, 0)
            grad = tiles(do_ref, rows, 0)
            lse = lse_ref[0, :, span]
            if side == 0:
                lse = lse + bad
            p = jnp.exp2(dot(key, query, NT) * BASE2 - lse)
            e = dot(sides[side][u, 0, 1], grad, NT)
            g = (p * (e - row_ref[:, span])).astype(jnp.bfloat16)
            dk = dot(g, query, NN) * SCALE
            dv = dot(p.astype(jnp.bfloat16), grad, NN)
            dqt_ref[:, span] += dot(key, g, TN)
            outs[side][u, 0, 0] = dk.astype(outs[side].dtype)
            outs[side][u, 0, 1] = dv.astype(outs[side].dtype)
    for b in range(ROWS):
        dq = dqt_ref[:, b * tokens : (b + 1) * tokens] * SCALE
        dq_ref[b, 0, 0] = dq.T.astype(jnp.bfloat16)


def heads_spec(first, count, tokens):
    return pl.BlockSpec((ROWS, 1, count, tokens, HEAD_DIM), lambda i: (0, first + i, 0, 0, 0))


def attend_backward(first, heads, bad, q, kv_other, kv, kv_partner, grad, mixed, lse, after):
    tokens = q.shape[3]
    return pl.pallas_call(
        backward_kernel,
        grid=(heads,),
        in_specs=[pl.BlockSpec(memory_space=pltpu.SMEM), heads_spec(first, 1, tokens)]
        + [heads_spec(first, 2, tokens)] * 3
        + [heads_spec(first, 1, tokens)] * 2
        + [pl.BlockSpec((1, 1, ROWS * tokens), lambda i: (first + i, 0, 0))]
        + [pl.BlockSpec(memory_space=pl.ANY)] * len(after),
        out_specs=[heads_spec(0, 1, tokens)] + [heads_spec(0, 2, tokens)] * 3,
        out_shape=[bf16(ROWS, heads, 1, tokens, HEAD_DIM)]
        + [bf16(ROWS, heads, 2, tokens, HEAD_DIM)] * 3,
        scratch_shapes=[
            pltpu.VMEM((HEAD_DIM, ROWS * tokens), jnp.float32),
            pltpu.VMEM((1, ROWS * tokens), jnp.float32),
        ],
        cost_estimate=cost(100),
        compiler_params=params(),
    )(bad, q, kv_other, kv, kv_partner, grad, mixed, lse, *after)


def add_terms(refs, row, head, tensor):
    terms = [ref[row, head, tensor].astype(jnp.float32) for ref in refs]
    return functools.reduce(jnp.add, terms).astype(jnp.bfloat16)


def early_kernel(dq_ref, *refs):
    terms, late_ref, out_ref = refs[:3], refs[3], refs[-1]
    for r in range(ROWS):
        out_ref[r, 0] = dq_ref[r, 0, 0]
        for t in range(2):
            out_ref[r, 1 + t] = add_terms(terms, r, 0, t)
        for h in range(late_ref.shape[1]):
            out_ref[r, 3 + h] = late_ref[r, h, 0]


def late_kernel(*refs):
    terms, out_ref = refs[:3], refs[-1]
    for r in range(ROWS):
        for h in range(terms[0].shape[1]):
            for t in range(2):
                out_ref[r, 2 * h + t] = add_terms(terms, r, h, t)


def totals(kernel, slots, arrays, after=(), told=0.1):
    tokens = arrays[0].shape[3]
    vmem = pl.BlockSpec(memory_space=pltpu.VMEM)
    return pl.pallas_call(
        kernel,
        in_specs=[vmem] * len(arrays) + [pl.BlockSpec(memory_space=pl.ANY)] * len(after),
        out_specs=vmem,
        out_shape=bf16(ROWS, slots, tokens, HEAD_DIM),
        cost_estimate=cost(told),
        compiler_params=params(),
    )(*arrays, *after)


def lane_sums(products):
    rows = products[0].shape[0]
    product = jnp.concatenate(products, axis=0)
    high = product.astype(jnp.bfloat16)
    low = (product - high.astype(jnp.float32)).astype(jnp.bfloat16)
    ones = jnp.ones((2 * HEAD_DIM, HEAD_DIM), jnp.bfloat16)
    sums = dot(jnp.concatenate([high, low], axis=1), ones, NN)
    return [sums[i * rows : (i + 1) * rows] for i in range(len(products))]


def temporal_weights(probes, anchors):
    scores = lane_sums([p * a for p in probes for a in anchors])
    weights = []
    for f in range(PARTS):
        row = [s * SCALE for s in scores[f * PARTS : (f + 1) * PARTS]]
        top = functools.reduce(jnp.maximum, row)
        shifted = [jnp.exp(s - top) for s in row]
        inverse = 1.0 / functools.reduce(jnp.add, shifted)
        weights.append([s * inverse for s in shifted])
    return weights


def rounded(x):
    return x.astype(jnp.bfloat16).astype(jnp.float32)


def temporal_forward_kernel(*refs):
    ins, outs = refs[:PARTS], refs[-PARTS:]
    parts = [[ref[0, t].astype(jnp.float32) for ref in ins] for t in range(3)]
    weights = temporal_weights(parts[0], parts[1])
    for g in range(PARTS):
        terms = [rounded(weights[f][g]) * parts[2][f] for f in range(PARTS)]
        outs[g][0, 0] = functools.reduce(jnp.add, terms).astype(jnp.bfloat16)


def temporal_backward_kernel(*refs):
    ins, mixed_refs, outs = refs[:PARTS], refs[PARTS : 2 * PARTS], refs[-PARTS:]
    parts = [[ref[0, t].astype(jnp.float32) for ref in ins] for t in range(3)]
    mixed = [ref[0, 0].astype(jnp.float32) for ref in mixed_refs]
    weights = temporal_weights(parts[0], parts[1])
    sums = lane_sums([u * m for u in parts[2] for m in mixed])
    anchor_grads = [None] * PARTS
    for f in range(PARTS):
        grads = sums[f * PARTS : (f + 1) * PARTS]
        row = functools.reduce(jnp.add, [w * c for w, c in zip(weights[f], grads)])
        scores = [rounded(w * (c - row)) for w, c in zip(weights[f], grads)]
        probe = functools.reduce(jnp.add, [s * parts[1][g] for g, s in enumerate(scores)])
        outs[f][0, 0] = (probe * SCALE).astype(jnp.bfloat16)
        for g in range(PARTS):
            term = scores[g] * parts[0][f]
            anchor_grads[g] = term if f == 0 else anchor_grads[g] + term
    for g in range(PARTS):
        outs[g][0, 1] = (anchor_grads[g] * SCALE).astype(jnp.bfloat16)


def temporal_call(kernel, arrays, count_out, told, after=()):
    group, _, tokens, _ = arrays[0].shape
    rows = 128

    def spec(count):
        return pl.BlockSpec((1, count, rows, HEAD_DIM), lambda h, i: (h, 0, i, 0))

    return pl.pallas_call(
        kernel,
        grid=(group, tokens // rows),
        in_specs=[spec(a.shape[1]) for a in arrays]
        + [pl.BlockSpec(memory_space=pl.ANY)] * len(after),
        out_specs=[spec(count_out)] * PARTS,
        out_shape=[bf16(group, count_out, tokens, HEAD_DIM)] * PARTS,
        cost_estimate=cost(told),
        compiler_params=params(),
    )(*arrays, *after)


def swap(x, axis):
    return lax.all_to_all(x, axis, split_axis=0, concat_axis=0, tiled=True)


def trade_partner(x):
    return lax.ppermute(x, "wa", [(i, i ^ 1) for i in range(lax.axis_size("wa"))])


def trade_other(x):
    firsts = range(1, lax.axis_size("wa") - 1, 2)
    pairs = [(i, i + 1) for i in firsts] + [(i + 1, i) for i in firsts]
    return lax.ppermute(x, "wa", pairs)


def shards(queries, tile_keys, values, probes, anchors, upstream):
    shape = queries.shape
    tokens = shape[2] * shape[3]

    def flat(x):
        return x.reshape(tokens, shape[-1])

    place = lax.axis_index("wa")
    no_other = (place == 0) | (place == lax.axis_size("wa") - 1)
    bad = no_other.astype(jnp.float32).reshape(1) * BIG

    kv_sent = pack([flat(tile_keys), flat(values)])
    kv = swap(kv_sent, "ha")
    kv_other = trade_other(kv)
    kv_partner = trade_partner(kv)
    pau_sent = pack_partners([flat(probes), flat(anchors), flat(upstream)], [kv_sent])
    pau = trade(pau_sent)
    q_sent = pack([flat(queries)], pau_sent[:1])
    q = swap(q_sent, "ha")
    grad_parts = trade(temporal_call(temporal_forward_kernel, pau, 1, 10, [kv, q_sent]))
    grad_sent = join_partners(grad_parts)
    grad = swap(grad_sent, "ha")
    mixed, lse = attend_forward(bad, q, kv_other, kv, kv_partner, grad_sent)
    mixed_sent = split_partners(swap(mixed, "ha"))
    mixed_parts = trade(mixed_sent)
    def backward(first, heads, after):
        dq, to_other, own, to_partner = attend_backward(
            first, heads, bad, q, kv_other, kv, kv_partner, grad, mixed, lse, after
        )
        return dq, own, trade_other(to_other), trade_partner(to_partner)

    one = backward(0, 1, [])
    two = backward(1, GROUP - 1, [mixed_sent[0], one[0]])
    early = totals(early_kernel, GROUP + 2, (*one, two[0]), told=0.1)
    times_sent = temporal_call(
        temporal_backward_kernel, pau + mixed_parts, 2, 5, [early]
    )
    early = swap(early, "ha")
    late = swap(totals(late_kernel, 2 * (GROUP - 1), two[1:], [early]), "ha")
    probe_grad, anchor_grad = unpack_partners(trade(times_sent), [])
    query_grad, key_grad, value_grad = unpack_heads(early, late)
    outs = (query_grad, key_grad, value_grad, probe_grad, anchor_grad)
    return tuple(x.reshape(shape) for x in outs)


def solution(mesh):
    spec = P(None, "tm", "ha", "wa", None)
    return jax.shard_map(
        shards,
        mesh=mesh,
        in_specs=(spec,) * 6,
        out_specs=(spec,) * 5,
        check_vma=False,
    )
```

```python
import functools

import jax
import jax.numpy as jnp
from jax import lax
from jax.experimental import pallas as pl
from jax.experimental.pallas import tpu as pltpu
from jax.sharding import PartitionSpec as P

HEADS = 12
HEAD_DIM = 128
PARTS = 4
GROUP = HEADS // PARTS
ROWS = 4
BIG = 1e30
SCALE = HEAD_DIM ** (-0.5)
LOG2E = 1.4426950408889634
BASE2 = SCALE * LOG2E

NT = (((1,), (1,)), ((), ()))
NN = (((1,), (0,)), ((), ()))
TN = (((0,), (0,)), ((), ()))


def dot(a, b, dims):
    return lax.dot_general(a, b, dims, preferred_element_type=jnp.float32)


def params():
    return pltpu.CompilerParams(vmem_limit_bytes=64 * 1024 * 1024)


def cost(microseconds):
    return pl.CostEstimate(
        flops=int(microseconds * 1e9), bytes_accessed=1024, transcendentals=0
    )


def move(inputs, out_shapes, plan, axis=None, after=(), told=0.1):
    first = len(inputs) + len(after)

    def kernel(*refs):
        ins = refs[: len(inputs)]
        outs = refs[first:]
        me = 0 if axis is None else lax.axis_index(axis)
        for i, at, o, to in plan(me):
            outs[o][to] = ins[i][at]

    return pl.pallas_call(
        kernel,
        in_specs=[pl.BlockSpec(memory_space=pltpu.VMEM)] * len(inputs)
        + [pl.BlockSpec(memory_space=pl.ANY)] * len(after),
        out_specs=[pl.BlockSpec(memory_space=pltpu.VMEM)] * len(out_shapes),
        out_shape=out_shapes,
        cost_estimate=cost(told),
        compiler_params=params(),
    )(*inputs, *after)


def columns(group, head):
    start = (group * GROUP + head) * HEAD_DIM
    if not isinstance(start, int):
        start = pl.multiple_of(start, HEAD_DIM)
    return (slice(None), pl.ds(start, HEAD_DIM))


def bf16(*shape):
    return jax.ShapeDtypeStruct(shape, jnp.bfloat16)


def pack(arrays, after=(), told=0.1):
    tokens = arrays[0].shape[0]
    cells = [(a, d, h) for d in range(PARTS) for h in range(GROUP) for a in range(len(arrays))]
    return move(
        arrays,
        [bf16(PARTS, GROUP, len(arrays), tokens, HEAD_DIM)],
        lambda me: [(a, columns(d, h), 0, (d, h, a)) for a, d, h in cells],
        after=after,
        told=told,
    )[0]


def pack_partners(arrays, after=()):
    tokens = arrays[0].shape[0]
    cells = [(a, s, h) for s in range(PARTS) for h in range(GROUP) for a in range(len(arrays))]
    return move(
        arrays,
        [bf16(GROUP, len(arrays), tokens, HEAD_DIM)] * PARTS,
        lambda me: [(a, columns(me ^ s, h), s, (h, a)) for a, s, h in cells],
        "tm",
        after,
    )


def unpack_partners(chunks, after):
    _, count, tokens, _ = chunks[0].shape
    cells = [(a, s, h) for s in range(PARTS) for h in range(GROUP) for a in range(count)]
    return move(
        chunks,
        [bf16(tokens, HEADS * HEAD_DIM)] * count,
        lambda me: [(s, (h, a), a, columns(me ^ s, h)) for a, s, h in cells],
        "tm",
        after,
        told=100,
    )


def join_partners(chunks):
    return move(
        chunks,
        [bf16(PARTS, *chunks[0].shape)],
        lambda me: [(s, (slice(None),), 0, (me ^ s,)) for s in range(PARTS)],
        "tm",
    )[0]


def split_partners(block):
    return move(
        [block],
        [bf16(*block.shape[1:])] * PARTS,
        lambda me: [(0, (me ^ s,), s, (slice(None),)) for s in range(PARTS)],
        "tm",
    )


def unpack_heads(early, late):
    tokens = early.shape[2]
    places = [[(0, 0), (0, 1), (0, 2)]]
    for h in range(GROUP - 1):
        places.append([(0, 3 + h), (1, 2 * h), (1, 2 * h + 1)])
    cells = [(a, d, h) for h in range(GROUP) for d in range(PARTS) for a in range(3)]
    return move(
        [early, late],
        [bf16(tokens, HEADS * HEAD_DIM)] * 3,
        lambda me: [
            (places[h][a][0], (d, places[h][a][1]), a, columns(d, h)) for a, d, h in cells
        ],
    )


def trade(chunks):
    out = [chunks[0]]
    for s in range(1, PARTS):
        out.append(lax.ppermute(chunks[s], "tm", [(i, i ^ s) for i in range(PARTS)]))
    return out


def near_rows(row):
    return max(row - 1, 0), min(row + 2, ROWS)


def tiles(ref, rows, tensor):
    low, high = rows
    block = ref[low:high, 0, tensor]
    return block.reshape((high - low) * block.shape[1], HEAD_DIM)


def forward_kernel(bad_ref, q_ref, other_ref, own_ref, partner_ref, _, o_ref, lse_ref, vt_ref):
    bad = bad_ref[0]
    sides = (other_ref, own_ref, partner_ref)
    tokens = q_ref.shape[3]
    for side in range(3):
        vt_ref[side] = tiles(sides[side], (0, ROWS), 1).T
    for b in range(ROWS):
        query = q_ref[b, 0, 0]
        rows = near_rows(b)
        span = slice(rows[0] * tokens, rows[1] * tokens)
        scores = [dot(tiles(ref, rows, 0), query, NT) for ref in sides]
        tops = [jnp.max(s, axis=0, keepdims=True) for s in scores]
        top = functools.reduce(jnp.maximum, [tops[0] - bad] + tops[1:]) * BASE2
        total = None
        mixed = None
        for side, s in enumerate(scores):
            p = jnp.exp2(s * BASE2 - (top + bad if side == 0 else top))
            one = jnp.sum(p, axis=0, keepdims=True)
            total = one if total is None else total + one
            term = dot(vt_ref[side, :, span], p.astype(jnp.bfloat16), NN)
            mixed = term if mixed is None else mixed + term
        mixed = mixed * (1.0 / total)
        o_ref[b, 0, 0] = mixed.T.astype(jnp.bfloat16)
        lse_ref[0, :, b * tokens : (b + 1) * tokens] = top + jnp.log2(total)


def column_spec(count, tokens):
    return pl.BlockSpec((ROWS, 1, count, tokens, HEAD_DIM), lambda h: (0, h, 0, 0, 0))


def attend_forward(bad, q, kv_other, kv, kv_partner, after):
    tokens = q.shape[3]
    group = q.shape[1]
    return pl.pallas_call(
        forward_kernel,
        grid=(group,),
        in_specs=[pl.BlockSpec(memory_space=pltpu.SMEM), column_spec(1, tokens)]
        + [column_spec(2, tokens)] * 3
        + [pl.BlockSpec(memory_space=pl.ANY)],
        out_specs=[
            column_spec(1, tokens),
            pl.BlockSpec((1, 1, ROWS * tokens), lambda h: (h, 0, 0)),
        ],
        out_shape=[
            jax.ShapeDtypeStruct(q.shape, jnp.bfloat16),
            jax.ShapeDtypeStruct((group, 1, ROWS * tokens), jnp.float32),
        ],
        scratch_shapes=[pltpu.VMEM((3, HEAD_DIM, ROWS * tokens), jnp.bfloat16)],
        cost_estimate=cost(100),
        compiler_params=params(),
    )(bad, q, kv_other, kv, kv_partner, after)


def backward_kernel(
    bad_ref, q_ref, other_ref, own_ref, partner_ref, do_ref, o_ref, lse_ref, *rest
):
    dq_ref, d_other_ref, d_own_ref, d_partner_ref, dqt_ref, row_ref = rest[-6:]
    bad = bad_ref[0]
    sides = (other_ref, own_ref, partner_ref)
    outs = (d_other_ref, d_own_ref, d_partner_ref)
    tokens = q_ref.shape[3]
    for b in range(ROWS):
        product = do_ref[b, 0, 0].astype(jnp.float32) * o_ref[b, 0, 0].astype(jnp.float32)
        row_ref[:, b * tokens : (b + 1) * tokens] = jnp.sum(product.T, axis=0, keepdims=True)
    dqt_ref[...] = jnp.zeros_like(dqt_ref)
    for side in range(3):
        for u in range(ROWS):
            rows = near_rows(u)
            span = slice(rows[0] * tokens, rows[1] * tokens)
            key = sides[side][u, 0, 0]
            query = tiles(q_ref, rows, 0)
            grad = tiles(do_ref, rows, 0)
            lse = lse_ref[0, :, span]
            if side == 0:
                lse = lse + bad
            p = jnp.exp2(dot(key, query, NT) * BASE2 - lse)
            e = dot(sides[side][u, 0, 1], grad, NT)
            g = (p * (e - row_ref[:, span])).astype(jnp.bfloat16)
            dk = dot(g, query, NN) * SCALE
            dv = dot(p.astype(jnp.bfloat16), grad, NN)
            dqt_ref[:, span] += dot(key, g, TN)
            outs[side][u, 0, 0] = dk.astype(outs[side].dtype)
            outs[side][u, 0, 1] = dv.astype(outs[side].dtype)
    for b in range(ROWS):
        dq = dqt_ref[:, b * tokens : (b + 1) * tokens] * SCALE
        dq_ref[b, 0, 0] = dq.T.astype(jnp.bfloat16)


def heads_spec(first, count, tokens):
    return pl.BlockSpec((ROWS, 1, count, tokens, HEAD_DIM), lambda i: (0, first + i, 0, 0, 0))


def attend_backward(first, heads, bad, q, kv_other, kv, kv_partner, grad, mixed, lse, after):
    tokens = q.shape[3]
    return pl.pallas_call(
        backward_kernel,
        grid=(heads,),
        in_specs=[pl.BlockSpec(memory_space=pltpu.SMEM), heads_spec(first, 1, tokens)]
        + [heads_spec(first, 2, tokens)] * 3
        + [heads_spec(first, 1, tokens)] * 2
        + [pl.BlockSpec((1, 1, ROWS * tokens), lambda i: (first + i, 0, 0))]
        + [pl.BlockSpec(memory_space=pl.ANY)] * len(after),
        out_specs=[heads_spec(0, 1, tokens)] + [heads_spec(0, 2, tokens)] * 3,
        out_shape=[bf16(ROWS, heads, 1, tokens, HEAD_DIM)]
        + [bf16(ROWS, heads, 2, tokens, HEAD_DIM)] * 3,
        scratch_shapes=[
            pltpu.VMEM((HEAD_DIM, ROWS * tokens), jnp.float32),
            pltpu.VMEM((1, ROWS * tokens), jnp.float32),
        ],
        cost_estimate=cost(100),
        compiler_params=params(),
    )(bad, q, kv_other, kv, kv_partner, grad, mixed, lse, *after)


def add_terms(refs, row, head, tensor):
    terms = [ref[row, head, tensor].astype(jnp.float32) for ref in refs]
    return functools.reduce(jnp.add, terms).astype(jnp.bfloat16)


def early_kernel(dq_ref, *refs):
    terms, late_ref, out_ref = refs[:3], refs[3], refs[-1]
    for r in range(ROWS):
        out_ref[r, 0] = dq_ref[r, 0, 0]
        for t in range(2):
            out_ref[r, 1 + t] = add_terms(terms, r, 0, t)
        for h in range(late_ref.shape[1]):
            out_ref[r, 3 + h] = late_ref[r, h, 0]


def late_kernel(*refs):
    terms, out_ref = refs[:3], refs[-1]
    for r in range(ROWS):
        for h in range(terms[0].shape[1]):
            for t in range(2):
                out_ref[r, 2 * h + t] = add_terms(terms, r, h, t)


def totals(kernel, slots, arrays, after=(), told=0.1):
    tokens = arrays[0].shape[3]
    vmem = pl.BlockSpec(memory_space=pltpu.VMEM)
    return pl.pallas_call(
        kernel,
        in_specs=[vmem] * len(arrays) + [pl.BlockSpec(memory_space=pl.ANY)] * len(after),
        out_specs=vmem,
        out_shape=bf16(ROWS, slots, tokens, HEAD_DIM),
        cost_estimate=cost(told),
        compiler_params=params(),
    )(*arrays, *after)


def lane_sums(products):
    rows = products[0].shape[0]
    product = jnp.concatenate(products, axis=0)
    high = product.astype(jnp.bfloat16)
    low = (product - high.astype(jnp.float32)).astype(jnp.bfloat16)
    ones = jnp.ones((2 * HEAD_DIM, HEAD_DIM), jnp.bfloat16)
    sums = dot(jnp.concatenate([high, low], axis=1), ones, NN)
    return [sums[i * rows : (i + 1) * rows] for i in range(len(products))]


def temporal_weights(probes, anchors):
    scores = lane_sums([p * a for p in probes for a in anchors])
    weights = []
    for f in range(PARTS):
        row = [s * SCALE for s in scores[f * PARTS : (f + 1) * PARTS]]
        top = functools.reduce(jnp.maximum, row)
        shifted = [jnp.exp(s - top) for s in row]
        inverse = 1.0 / functools.reduce(jnp.add, shifted)
        weights.append([s * inverse for s in shifted])
    return weights


def rounded(x):
    return x.astype(jnp.bfloat16).astype(jnp.float32)


def temporal_forward_kernel(*refs):
    ins, outs = refs[:PARTS], refs[-PARTS:]
    parts = [[ref[0, t].astype(jnp.float32) for ref in ins] for t in range(3)]
    weights = temporal_weights(parts[0], parts[1])
    for g in range(PARTS):
        terms = [rounded(weights[f][g]) * parts[2][f] for f in range(PARTS)]
        outs[g][0, 0] = functools.reduce(jnp.add, terms).astype(jnp.bfloat16)


def temporal_backward_kernel(*refs):
    ins, mixed_refs, outs = refs[:PARTS], refs[PARTS : 2 * PARTS], refs[-PARTS:]
    parts = [[ref[0, t].astype(jnp.float32) for ref in ins] for t in range(3)]
    mixed = [ref[0, 0].astype(jnp.float32) for ref in mixed_refs]
    weights = temporal_weights(parts[0], parts[1])
    sums = lane_sums([u * m for u in parts[2] for m in mixed])
    anchor_grads = [None] * PARTS
    for f in range(PARTS):
        grads = sums[f * PARTS : (f + 1) * PARTS]
        row = functools.reduce(jnp.add, [w * c for w, c in zip(weights[f], grads)])
        scores = [rounded(w * (c - row)) for w, c in zip(weights[f], grads)]
        probe = functools.reduce(jnp.add, [s * parts[1][g] for g, s in enumerate(scores)])
        outs[f][0, 0] = (probe * SCALE).astype(jnp.bfloat16)
        for g in range(PARTS):
            term = scores[g] * parts[0][f]
            anchor_grads[g] = term if f == 0 else anchor_grads[g] + term
    for g in range(PARTS):
        outs[g][0, 1] = (anchor_grads[g] * SCALE).astype(jnp.bfloat16)


def temporal_call(kernel, arrays, count_out, told, after=()):
    group, _, tokens, _ = arrays[0].shape
    rows = 128

    def spec(count):
        return pl.BlockSpec((1, count, rows, HEAD_DIM), lambda h, i: (h, 0, i, 0))

    return pl.pallas_call(
        kernel,
        grid=(group, tokens // rows),
        in_specs=[spec(a.shape[1]) for a in arrays]
        + [pl.BlockSpec(memory_space=pl.ANY)] * len(after),
        out_specs=[spec(count_out)] * PARTS,
        out_shape=[bf16(group, count_out, tokens, HEAD_DIM)] * PARTS,
        cost_estimate=cost(told),
        compiler_params=params(),
    )(*arrays, *after)


def swap(x, axis):
    return lax.all_to_all(x, axis, split_axis=0, concat_axis=0, tiled=True)


def trade_partner(x):
    return lax.ppermute(x, "wa", [(i, i ^ 1) for i in range(lax.axis_size("wa"))])


def trade_other(x):
    firsts = range(1, lax.axis_size("wa") - 1, 2)
    pairs = [(i, i + 1) for i in firsts] + [(i + 1, i) for i in firsts]
    return lax.ppermute(x, "wa", pairs)


def shards(queries, tile_keys, values, probes, anchors, upstream):
    shape = queries.shape
    tokens = shape[2] * shape[3]

    def flat(x):
        return x.reshape(tokens, shape[-1])

    place = lax.axis_index("wa")
    no_other = (place == 0) | (place == lax.axis_size("wa") - 1)
    bad = no_other.astype(jnp.float32).reshape(1) * BIG

    kv_sent = pack([flat(tile_keys), flat(values)])
    kv = swap(kv_sent, "ha")
    kv_other = trade_other(kv)
    kv_partner = trade_partner(kv)
    pau_sent = pack_partners([flat(probes), flat(anchors), flat(upstream)], [kv_sent])
    pau = trade(pau_sent)
    q_sent = pack([flat(queries)], pau_sent[:1])
    q = swap(q_sent, "ha")
    grad_parts = trade(temporal_call(temporal_forward_kernel, pau, 1, 10, [kv, q_sent]))
    grad_sent = join_partners(grad_parts)
    grad = swap(grad_sent, "ha")
    mixed, lse = attend_forward(bad, q, kv_other, kv, kv_partner, grad_sent)
    mixed_sent = split_partners(swap(mixed, "ha"))
    mixed_parts = trade(mixed_sent)
    def backward(first, heads, after):
        dq, to_other, own, to_partner = attend_backward(
            first, heads, bad, q, kv_other, kv, kv_partner, grad, mixed, lse, after
        )
        return dq, own, trade_other(to_other), trade_partner(to_partner)

    one = backward(0, 1, [])
    two = backward(1, GROUP - 1, [mixed_sent[0], one[0]])
    early = totals(early_kernel, GROUP + 2, (*one, two[0]), told=0.1)
    times_sent = temporal_call(
        temporal_backward_kernel, pau + mixed_parts, 2, 5, [early]
    )
    early = swap(early, "ha")
    late = swap(totals(late_kernel, 2 * (GROUP - 1), two[1:], [early]), "ha")
    probe_grad, anchor_grad = unpack_partners(trade(times_sent), [])
    query_grad, key_grad, value_grad = unpack_heads(early, late)
    outs = (query_grad, key_grad, value_grad, probe_grad, anchor_grad)
    return tuple(x.reshape(shape) for x in outs)


def solution(mesh):
    spec = P(None, "tm", "ha", "wa", None)
    return jax.shard_map(
        shards,
        mesh=mesh,
        in_specs=(spec,) * 6,
        out_specs=(spec,) * 5,
        check_vma=False,
    )
```

```python
import functools

import jax
import jax.numpy as jnp
from jax import lax
from jax.experimental import pallas as pl
from jax.experimental.pallas import tpu as pltpu
from jax.sharding import PartitionSpec as P

HEADS = 12
HEAD_DIM = 128
PARTS = 4
GROUP = HEADS // PARTS
ROWS = 4
BIG = 1e30
SCALE = HEAD_DIM ** (-0.5)
LOG2E = 1.4426950408889634
BASE2 = SCALE * LOG2E

NT = (((1,), (1,)), ((), ()))
NN = (((1,), (0,)), ((), ()))
TN = (((0,), (0,)), ((), ()))


def dot(a, b, dims):
    return lax.dot_general(a, b, dims, preferred_element_type=jnp.float32)


def params():
    return pltpu.CompilerParams(vmem_limit_bytes=64 * 1024 * 1024)


def cost(microseconds):
    return pl.CostEstimate(
        flops=int(microseconds * 1e9), bytes_accessed=1024, transcendentals=0
    )


def move(inputs, out_shapes, plan, axis=None, after=(), told=0.1):
    first = len(inputs) + len(after)

    def kernel(*refs):
        ins = refs[: len(inputs)]
        outs = refs[first:]
        me = 0 if axis is None else lax.axis_index(axis)
        for i, at, o, to in plan(me):
            outs[o][to] = ins[i][at]

    return pl.pallas_call(
        kernel,
        in_specs=[pl.BlockSpec(memory_space=pltpu.VMEM)] * len(inputs)
        + [pl.BlockSpec(memory_space=pl.ANY)] * len(after),
        out_specs=[pl.BlockSpec(memory_space=pltpu.VMEM)] * len(out_shapes),
        out_shape=out_shapes,
        cost_estimate=cost(told),
        compiler_params=params(),
    )(*inputs, *after)


def columns(group, head):
    start = (group * GROUP + head) * HEAD_DIM
    if not isinstance(start, int):
        start = pl.multiple_of(start, HEAD_DIM)
    return (slice(None), pl.ds(start, HEAD_DIM))


def bf16(*shape):
    return jax.ShapeDtypeStruct(shape, jnp.bfloat16)


def pack(arrays, after=(), told=0.1):
    tokens = arrays[0].shape[0]
    cells = [(a, d, h) for d in range(PARTS) for h in range(GROUP) for a in range(len(arrays))]
    return move(
        arrays,
        [bf16(PARTS, GROUP, len(arrays), tokens, HEAD_DIM)],
        lambda me: [(a, columns(d, h), 0, (d, h, a)) for a, d, h in cells],
        after=after,
        told=told,
    )[0]


def pack_partners(arrays, after=()):
    tokens = arrays[0].shape[0]
    cells = [(a, s, h) for s in range(PARTS) for h in range(GROUP) for a in range(len(arrays))]
    return move(
        arrays,
        [bf16(GROUP, len(arrays), tokens, HEAD_DIM)] * PARTS,
        lambda me: [(a, columns(me ^ s, h), s, (h, a)) for a, s, h in cells],
        "tm",
        after,
    )


def unpack_partners(chunks, after):
    _, count, tokens, _ = chunks[0].shape
    cells = [(a, s, h) for s in range(PARTS) for h in range(GROUP) for a in range(count)]
    return move(
        chunks,
        [bf16(tokens, HEADS * HEAD_DIM)] * count,
        lambda me: [(s, (h, a), a, columns(me ^ s, h)) for a, s, h in cells],
        "tm",
        after,
        told=100,
    )


def join_partners(chunks):
    return move(
        chunks,
        [bf16(PARTS, *chunks[0].shape)],
        lambda me: [(s, (slice(None),), 0, (me ^ s,)) for s in range(PARTS)],
        "tm",
    )[0]


def split_partners(block):
    return move(
        [block],
        [bf16(*block.shape[1:])] * PARTS,
        lambda me: [(0, (me ^ s,), s, (slice(None),)) for s in range(PARTS)],
        "tm",
    )


def unpack_heads(early, late):
    tokens = early.shape[2]
    places = [[(0, 0), (0, 1), (0, 2)]]
    for h in range(GROUP - 1):
        places.append([(0, 3 + h), (1, 2 * h), (1, 2 * h + 1)])
    cells = [(a, d, h) for h in range(GROUP) for d in range(PARTS) for a in range(3)]
    return move(
        [early, late],
        [bf16(tokens, HEADS * HEAD_DIM)] * 3,
        lambda me: [
            (places[h][a][0], (d, places[h][a][1]), a, columns(d, h)) for a, d, h in cells
        ],
    )


def trade(chunks):
    out = [chunks[0]]
    for s in range(1, PARTS):
        out.append(lax.ppermute(chunks[s], "tm", [(i, i ^ s) for i in range(PARTS)]))
    return out


def near_rows(row):
    return max(row - 1, 0), min(row + 2, ROWS)


def tiles(ref, rows, tensor):
    low, high = rows
    block = ref[low:high, 0, tensor]
    return block.reshape((high - low) * block.shape[1], HEAD_DIM)


def forward_kernel(bad_ref, q_ref, other_ref, own_ref, partner_ref, _, o_ref, lse_ref, vt_ref):
    bad = bad_ref[0]
    sides = (other_ref, own_ref, partner_ref)
    tokens = q_ref.shape[3]
    for side in range(3):
        vt_ref[side] = tiles(sides[side], (0, ROWS), 1).T
    for b in range(ROWS):
        query = q_ref[b, 0, 0]
        rows = near_rows(b)
        span = slice(rows[0] * tokens, rows[1] * tokens)
        scores = [dot(tiles(ref, rows, 0), query, NT) for ref in sides]
        tops = [jnp.max(s, axis=0, keepdims=True) for s in scores]
        top = functools.reduce(jnp.maximum, [tops[0] - bad] + tops[1:]) * BASE2
        total = None
        mixed = None
        for side, s in enumerate(scores):
            p = jnp.exp2(s * BASE2 - (top + bad if side == 0 else top))
            one = jnp.sum(p, axis=0, keepdims=True)
            total = one if total is None else total + one
            term = dot(vt_ref[side, :, span], p.astype(jnp.bfloat16), NN)
            mixed = term if mixed is None else mixed + term
        mixed = mixed * (1.0 / total)
        o_ref[b, 0, 0] = mixed.T.astype(jnp.bfloat16)
        lse_ref[0, :, b * tokens : (b + 1) * tokens] = top + jnp.log2(total)


def column_spec(count, tokens):
    return pl.BlockSpec((ROWS, 1, count, tokens, HEAD_DIM), lambda h: (0, h, 0, 0, 0))


def attend_forward(bad, q, kv_other, kv, kv_partner, after):
    tokens = q.shape[3]
    group = q.shape[1]
    return pl.pallas_call(
        forward_kernel,
        grid=(group,),
        in_specs=[pl.BlockSpec(memory_space=pltpu.SMEM), column_spec(1, tokens)]
        + [column_spec(2, tokens)] * 3
        + [pl.BlockSpec(memory_space=pl.ANY)],
        out_specs=[
            column_spec(1, tokens),
            pl.BlockSpec((1, 1, ROWS * tokens), lambda h: (h, 0, 0)),
        ],
        out_shape=[
            jax.ShapeDtypeStruct(q.shape, jnp.bfloat16),
            jax.ShapeDtypeStruct((group, 1, ROWS * tokens), jnp.float32),
        ],
        scratch_shapes=[pltpu.VMEM((3, HEAD_DIM, ROWS * tokens), jnp.bfloat16)],
        cost_estimate=cost(100),
        compiler_params=params(),
    )(bad, q, kv_other, kv, kv_partner, after)


def backward_kernel(
    bad_ref, q_ref, other_ref, own_ref, partner_ref, do_ref, o_ref, lse_ref, *rest
):
    dq_ref, d_other_ref, d_own_ref, d_partner_ref, dqt_ref, row_ref = rest[-6:]
    bad = bad_ref[0]
    sides = (other_ref, own_ref, partner_ref)
    outs = (d_other_ref, d_own_ref, d_partner_ref)
    tokens = q_ref.shape[3]
    for b in range(ROWS):
        product = do_ref[b, 0, 0].astype(jnp.float32) * o_ref[b, 0, 0].astype(jnp.float32)
        row_ref[:, b * tokens : (b + 1) * tokens] = jnp.sum(product.T, axis=0, keepdims=True)
    dqt_ref[...] = jnp.zeros_like(dqt_ref)
    for side in range(3):
        for u in range(ROWS):
            rows = near_rows(u)
            span = slice(rows[0] * tokens, rows[1] * tokens)
            key = sides[side][u, 0, 0]
            query = tiles(q_ref, rows, 0)
            grad = tiles(do_ref, rows, 0)
            lse = lse_ref[0, :, span]
            if side == 0:
                lse = lse + bad
            p = jnp.exp2(dot(key, query, NT) * BASE2 - lse)
            e = dot(sides[side][u, 0, 1], grad, NT)
            g = (p * (e - row_ref[:, span])).astype(jnp.bfloat16)
            dk = dot(g, query, NN) * SCALE
            dv = dot(p.astype(jnp.bfloat16), grad, NN)
            dqt_ref[:, span] += dot(key, g, TN)
            outs[side][u, 0, 0] = dk.astype(outs[side].dtype)
            outs[side][u, 0, 1] = dv.astype(outs[side].dtype)
    for b in range(ROWS):
        dq = dqt_ref[:, b * tokens : (b + 1) * tokens] * SCALE
        dq_ref[b, 0, 0] = dq.T.astype(jnp.bfloat16)


def heads_spec(first, count, tokens):
    return pl.BlockSpec((ROWS, 1, count, tokens, HEAD_DIM), lambda i: (0, first + i, 0, 0, 0))


def attend_backward(first, heads, bad, q, kv_other, kv, kv_partner, grad, mixed, lse, after):
    tokens = q.shape[3]
    return pl.pallas_call(
        backward_kernel,
        grid=(heads,),
        in_specs=[pl.BlockSpec(memory_space=pltpu.SMEM), heads_spec(first, 1, tokens)]
        + [heads_spec(first, 2, tokens)] * 3
        + [heads_spec(first, 1, tokens)] * 2
        + [pl.BlockSpec((1, 1, ROWS * tokens), lambda i: (first + i, 0, 0))]
        + [pl.BlockSpec(memory_space=pl.ANY)] * len(after),
        out_specs=[heads_spec(0, 1, tokens)] + [heads_spec(0, 2, tokens)] * 3,
        out_shape=[bf16(ROWS, heads, 1, tokens, HEAD_DIM)]
        + [bf16(ROWS, heads, 2, tokens, HEAD_DIM)] * 3,
        scratch_shapes=[
            pltpu.VMEM((HEAD_DIM, ROWS * tokens), jnp.float32),
            pltpu.VMEM((1, ROWS * tokens), jnp.float32),
        ],
        cost_estimate=cost(100),
        compiler_params=params(),
    )(bad, q, kv_other, kv, kv_partner, grad, mixed, lse, *after)


def add_terms(refs, row, head, tensor):
    terms = [ref[row, head, tensor].astype(jnp.float32) for ref in refs]
    return functools.reduce(jnp.add, terms).astype(jnp.bfloat16)


def early_kernel(dq_ref, *refs):
    terms, late_ref, out_ref = refs[:3], refs[3], refs[-1]
    for r in range(ROWS):
        out_ref[r, 0] = dq_ref[r, 0, 0]
        for t in range(2):
            out_ref[r, 1 + t] = add_terms(terms, r, 0, t)
        for h in range(late_ref.shape[1]):
            out_ref[r, 3 + h] = late_ref[r, h, 0]


def late_kernel(*refs):
    terms, out_ref = refs[:3], refs[-1]
    for r in range(ROWS):
        for h in range(terms[0].shape[1]):
            for t in range(2):
                out_ref[r, 2 * h + t] = add_terms(terms, r, h, t)


def totals(kernel, slots, arrays, after=(), told=0.1):
    tokens = arrays[0].shape[3]
    vmem = pl.BlockSpec(memory_space=pltpu.VMEM)
    return pl.pallas_call(
        kernel,
        in_specs=[vmem] * len(arrays) + [pl.BlockSpec(memory_space=pl.ANY)] * len(after),
        out_specs=vmem,
        out_shape=bf16(ROWS, slots, tokens, HEAD_DIM),
        cost_estimate=cost(told),
        compiler_params=params(),
    )(*arrays, *after)


def lane_sums(products):
    rows = products[0].shape[0]
    product = jnp.concatenate(products, axis=0)
    high = product.astype(jnp.bfloat16)
    low = (product - high.astype(jnp.float32)).astype(jnp.bfloat16)
    ones = jnp.ones((2 * HEAD_DIM, HEAD_DIM), jnp.bfloat16)
    sums = dot(jnp.concatenate([high, low], axis=1), ones, NN)
    return [sums[i * rows : (i + 1) * rows] for i in range(len(products))]


def temporal_weights(probes, anchors):
    scores = lane_sums([p * a for p in probes for a in anchors])
    weights = []
    for f in range(PARTS):
        row = [s * SCALE for s in scores[f * PARTS : (f + 1) * PARTS]]
        top = functools.reduce(jnp.maximum, row)
        shifted = [jnp.exp(s - top) for s in row]
        inverse = 1.0 / functools.reduce(jnp.add, shifted)
        weights.append([s * inverse for s in shifted])
    return weights


def rounded(x):
    return x.astype(jnp.bfloat16).astype(jnp.float32)


def temporal_forward_kernel(*refs):
    ins, outs = refs[:PARTS], refs[-PARTS:]
    parts = [[ref[0, t].astype(jnp.float32) for ref in ins] for t in range(3)]
    weights = temporal_weights(parts[0], parts[1])
    for g in range(PARTS):
        terms = [rounded(weights[f][g]) * parts[2][f] for f in range(PARTS)]
        outs[g][0, 0] = functools.reduce(jnp.add, terms).astype(jnp.bfloat16)


def temporal_backward_kernel(*refs):
    ins, mixed_refs, outs = refs[:PARTS], refs[PARTS : 2 * PARTS], refs[-PARTS:]
    parts = [[ref[0, t].astype(jnp.float32) for ref in ins] for t in range(3)]
    mixed = [ref[0, 0].astype(jnp.float32) for ref in mixed_refs]
    weights = temporal_weights(parts[0], parts[1])
    sums = lane_sums([u * m for u in parts[2] for m in mixed])
    anchor_grads = [None] * PARTS
    for f in range(PARTS):
        grads = sums[f * PARTS : (f + 1) * PARTS]
        row = functools.reduce(jnp.add, [w * c for w, c in zip(weights[f], grads)])
        scores = [rounded(w * (c - row)) for w, c in zip(weights[f], grads)]
        probe = functools.reduce(jnp.add, [s * parts[1][g] for g, s in enumerate(scores)])
        outs[f][0, 0] = (probe * SCALE).astype(jnp.bfloat16)
        for g in range(PARTS):
            term = scores[g] * parts[0][f]
            anchor_grads[g] = term if f == 0 else anchor_grads[g] + term
    for g in range(PARTS):
        outs[g][0, 1] = (anchor_grads[g] * SCALE).astype(jnp.bfloat16)


def temporal_call(kernel, arrays, count_out, told, after=()):
    group, _, tokens, _ = arrays[0].shape
    rows = 128

    def spec(count):
        return pl.BlockSpec((1, count, rows, HEAD_DIM), lambda h, i: (h, 0, i, 0))

    return pl.pallas_call(
        kernel,
        grid=(group, tokens // rows),
        in_specs=[spec(a.shape[1]) for a in arrays]
        + [pl.BlockSpec(memory_space=pl.ANY)] * len(after),
        out_specs=[spec(count_out)] * PARTS,
        out_shape=[bf16(group, count_out, tokens, HEAD_DIM)] * PARTS,
        cost_estimate=cost(told),
        compiler_params=params(),
    )(*arrays, *after)


def swap(x, axis):
    return lax.all_to_all(x, axis, split_axis=0, concat_axis=0, tiled=True)


def trade_partner(x):
    return lax.ppermute(x, "wa", [(i, i ^ 1) for i in range(lax.axis_size("wa"))])


def trade_other(x):
    firsts = range(1, lax.axis_size("wa") - 1, 2)
    pairs = [(i, i + 1) for i in firsts] + [(i + 1, i) for i in firsts]
    return lax.ppermute(x, "wa", pairs)


def shards(queries, tile_keys, values, probes, anchors, upstream):
    shape = queries.shape
    tokens = shape[2] * shape[3]

    def flat(x):
        return x.reshape(tokens, shape[-1])

    place = lax.axis_index("wa")
    no_other = (place == 0) | (place == lax.axis_size("wa") - 1)
    bad = no_other.astype(jnp.float32).reshape(1) * BIG

    kv_sent = pack([flat(tile_keys), flat(values)])
    kv = swap(kv_sent, "ha")
    kv_other = trade_other(kv)
    kv_partner = trade_partner(kv)
    pau_sent = pack_partners([flat(probes), flat(anchors), flat(upstream)], [kv_sent])
    pau = trade(pau_sent)
    q_sent = pack([flat(queries)], pau_sent[:1])
    q = swap(q_sent, "ha")
    grad_parts = trade(temporal_call(temporal_forward_kernel, pau, 1, 10, [kv, q_sent]))
    grad_sent = join_partners(grad_parts)
    grad = swap(grad_sent, "ha")
    mixed, lse = attend_forward(bad, q, kv_other, kv, kv_partner, grad_sent)
    mixed_sent = split_partners(swap(mixed, "ha"))
    mixed_parts = trade(mixed_sent)
    def backward(first, heads, after):
        dq, to_other, own, to_partner = attend_backward(
            first, heads, bad, q, kv_other, kv, kv_partner, grad, mixed, lse, after
        )
        return dq, own, trade_other(to_other), trade_partner(to_partner)

    one = backward(0, 1, [])
    two = backward(1, GROUP - 1, [mixed_sent[0], one[0]])
    early = totals(early_kernel, GROUP + 2, (*one, two[0]), told=0.1)
    times_sent = temporal_call(
        temporal_backward_kernel, pau + mixed_parts, 2, 5, [early]
    )
    early = swap(early, "ha")
    late = swap(totals(late_kernel, 2 * (GROUP - 1), two[1:], times_sent[:1]), "ha")
    probe_grad, anchor_grad = unpack_partners(trade(times_sent), [])
    query_grad, key_grad, value_grad = unpack_heads(early, late)
    outs = (query_grad, key_grad, value_grad, probe_grad, anchor_grad)
    return tuple(x.reshape(shape) for x in outs)


def solution(mesh):
    spec = P(None, "tm", "ha", "wa", None)
    return jax.shard_map(
        shards,
        mesh=mesh,
        in_specs=(spec,) * 6,
        out_specs=(spec,) * 5,
        check_vma=False,
    )
```

```python
import functools

import jax
import jax.numpy as jnp
from jax import lax
from jax.experimental import pallas as pl
from jax.experimental.pallas import tpu as pltpu
from jax.sharding import PartitionSpec as P

HEADS = 12
HEAD_DIM = 128
PARTS = 4
GROUP = HEADS // PARTS
ROWS = 4
BIG = 1e30
SCALE = HEAD_DIM ** (-0.5)
LOG2E = 1.4426950408889634
BASE2 = SCALE * LOG2E

NT = (((1,), (1,)), ((), ()))
NN = (((1,), (0,)), ((), ()))
TN = (((0,), (0,)), ((), ()))


def dot(a, b, dims):
    return lax.dot_general(a, b, dims, preferred_element_type=jnp.float32)


def params():
    return pltpu.CompilerParams(vmem_limit_bytes=64 * 1024 * 1024)


def cost(microseconds):
    return pl.CostEstimate(
        flops=int(microseconds * 1e9), bytes_accessed=1024, transcendentals=0
    )


def move(inputs, out_shapes, plan, axis=None, after=(), told=0.1):
    first = len(inputs) + len(after)

    def kernel(*refs):
        ins = refs[: len(inputs)]
        outs = refs[first:]
        me = 0 if axis is None else lax.axis_index(axis)
        for i, at, o, to in plan(me):
            outs[o][to] = ins[i][at]

    return pl.pallas_call(
        kernel,
        in_specs=[pl.BlockSpec(memory_space=pltpu.VMEM)] * len(inputs)
        + [pl.BlockSpec(memory_space=pl.ANY)] * len(after),
        out_specs=[pl.BlockSpec(memory_space=pltpu.VMEM)] * len(out_shapes),
        out_shape=out_shapes,
        cost_estimate=cost(told),
        compiler_params=params(),
    )(*inputs, *after)


def columns(group, head):
    start = (group * GROUP + head) * HEAD_DIM
    if not isinstance(start, int):
        start = pl.multiple_of(start, HEAD_DIM)
    return (slice(None), pl.ds(start, HEAD_DIM))


def bf16(*shape):
    return jax.ShapeDtypeStruct(shape, jnp.bfloat16)


def pack(arrays, after=(), told=0.1):
    tokens = arrays[0].shape[0]
    cells = [(a, d, h) for d in range(PARTS) for h in range(GROUP) for a in range(len(arrays))]
    return move(
        arrays,
        [bf16(PARTS, GROUP, len(arrays), tokens, HEAD_DIM)],
        lambda me: [(a, columns(d, h), 0, (d, h, a)) for a, d, h in cells],
        after=after,
        told=told,
    )[0]


def pack_partners(arrays, after=()):
    tokens = arrays[0].shape[0]
    cells = [(a, s, h) for s in range(PARTS) for h in range(GROUP) for a in range(len(arrays))]
    return move(
        arrays,
        [bf16(GROUP, len(arrays), tokens, HEAD_DIM)] * PARTS,
        lambda me: [(a, columns(me ^ s, h), s, (h, a)) for a, s, h in cells],
        "tm",
        after,
    )


def unpack_partners(chunks, after):
    _, count, tokens, _ = chunks[0].shape
    cells = [(a, s, h) for s in range(PARTS) for h in range(GROUP) for a in range(count)]
    return move(
        chunks,
        [bf16(tokens, HEADS * HEAD_DIM)] * count,
        lambda me: [(s, (h, a), a, columns(me ^ s, h)) for a, s, h in cells],
        "tm",
        after,
        told=100,
    )


def join_partners(chunks):
    return move(
        chunks,
        [bf16(PARTS, *chunks[0].shape)],
        lambda me: [(s, (slice(None),), 0, (me ^ s,)) for s in range(PARTS)],
        "tm",
    )[0]


def split_partners(block):
    return move(
        [block],
        [bf16(*block.shape[1:])] * PARTS,
        lambda me: [(0, (me ^ s,), s, (slice(None),)) for s in range(PARTS)],
        "tm",
    )


def unpack_heads(early, late):
    tokens = early.shape[2]
    places = [[(0, 0), (0, 1), (0, 2)]]
    for h in range(GROUP - 1):
        places.append([(0, 3 + h), (1, 2 * h), (1, 2 * h + 1)])
    cells = [(a, d, h) for h in range(GROUP) for d in range(PARTS) for a in range(3)]
    return move(
        [early, late],
        [bf16(tokens, HEADS * HEAD_DIM)] * 3,
        lambda me: [
            (places[h][a][0], (d, places[h][a][1]), a, columns(d, h)) for a, d, h in cells
        ],
    )


def trade(chunks):
    out = [chunks[0]]
    for s in range(1, PARTS):
        out.append(lax.ppermute(chunks[s], "tm", [(i, i ^ s) for i in range(PARTS)]))
    return out


def near_rows(row):
    return max(row - 1, 0), min(row + 2, ROWS)


def tiles(ref, rows, tensor):
    low, high = rows
    block = ref[low:high, 0, tensor]
    return block.reshape((high - low) * block.shape[1], HEAD_DIM)


def forward_kernel(bad_ref, q_ref, other_ref, own_ref, partner_ref, _, o_ref, lse_ref, vt_ref):
    bad = bad_ref[0]
    sides = (other_ref, own_ref, partner_ref)
    tokens = q_ref.shape[3]
    for side in range(3):
        vt_ref[side] = tiles(sides[side], (0, ROWS), 1).T
    for b in range(ROWS):
        query = q_ref[b, 0, 0]
        rows = near_rows(b)
        span = slice(rows[0] * tokens, rows[1] * tokens)
        scores = [dot(tiles(ref, rows, 0), query, NT) for ref in sides]
        tops = [jnp.max(s, axis=0, keepdims=True) for s in scores]
        top = functools.reduce(jnp.maximum, [tops[0] - bad] + tops[1:]) * BASE2
        total = None
        mixed = None
        for side, s in enumerate(scores):
            p = jnp.exp2(s * BASE2 - (top + bad if side == 0 else top))
            one = jnp.sum(p, axis=0, keepdims=True)
            total = one if total is None else total + one
            term = dot(vt_ref[side, :, span], p.astype(jnp.bfloat16), NN)
            mixed = term if mixed is None else mixed + term
        mixed = mixed * (1.0 / total)
        o_ref[b, 0, 0] = mixed.T.astype(jnp.bfloat16)
        lse_ref[0, :, b * tokens : (b + 1) * tokens] = top + jnp.log2(total)


def column_spec(count, tokens):
    return pl.BlockSpec((ROWS, 1, count, tokens, HEAD_DIM), lambda h: (0, h, 0, 0, 0))


def attend_forward(bad, q, kv_other, kv, kv_partner, after):
    tokens = q.shape[3]
    group = q.shape[1]
    return pl.pallas_call(
        forward_kernel,
        grid=(group,),
        in_specs=[pl.BlockSpec(memory_space=pltpu.SMEM), column_spec(1, tokens)]
        + [column_spec(2, tokens)] * 3
        + [pl.BlockSpec(memory_space=pl.ANY)],
        out_specs=[
            column_spec(1, tokens),
            pl.BlockSpec((1, 1, ROWS * tokens), lambda h: (h, 0, 0)),
        ],
        out_shape=[
            jax.ShapeDtypeStruct(q.shape, jnp.bfloat16),
            jax.ShapeDtypeStruct((group, 1, ROWS * tokens), jnp.float32),
        ],
        scratch_shapes=[pltpu.VMEM((3, HEAD_DIM, ROWS * tokens), jnp.bfloat16)],
        cost_estimate=cost(100),
        compiler_params=params(),
    )(bad, q, kv_other, kv, kv_partner, after)


def backward_kernel(
    bad_ref, q_ref, other_ref, own_ref, partner_ref, do_ref, o_ref, lse_ref, *rest
):
    dq_ref, d_other_ref, d_own_ref, d_partner_ref, dqt_ref, row_ref = rest[-6:]
    bad = bad_ref[0]
    sides = (other_ref, own_ref, partner_ref)
    outs = (d_other_ref, d_own_ref, d_partner_ref)
    tokens = q_ref.shape[3]
    for b in range(ROWS):
        product = do_ref[b, 0, 0].astype(jnp.float32) * o_ref[b, 0, 0].astype(jnp.float32)
        row_ref[:, b * tokens : (b + 1) * tokens] = jnp.sum(product.T, axis=0, keepdims=True)
    dqt_ref[...] = jnp.zeros_like(dqt_ref)
    for side in range(3):
        for u in range(ROWS):
            rows = near_rows(u)
            span = slice(rows[0] * tokens, rows[1] * tokens)
            key = sides[side][u, 0, 0]
            query = tiles(q_ref, rows, 0)
            grad = tiles(do_ref, rows, 0)
            lse = lse_ref[0, :, span]
            if side == 0:
                lse = lse + bad
            p = jnp.exp2(dot(key, query, NT) * BASE2 - lse)
            e = dot(sides[side][u, 0, 1], grad, NT)
            g = (p * (e - row_ref[:, span])).astype(jnp.bfloat16)
            dk = dot(g, query, NN) * SCALE
            dv = dot(p.astype(jnp.bfloat16), grad, NN)
            dqt_ref[:, span] += dot(key, g, TN)
            outs[side][u, 0, 0] = dk.astype(outs[side].dtype)
            outs[side][u, 0, 1] = dv.astype(outs[side].dtype)
    for b in range(ROWS):
        dq = dqt_ref[:, b * tokens : (b + 1) * tokens] * SCALE
        dq_ref[b, 0, 0] = dq.T.astype(jnp.bfloat16)


def heads_spec(first, count, tokens):
    return pl.BlockSpec((ROWS, 1, count, tokens, HEAD_DIM), lambda i: (0, first + i, 0, 0, 0))


def attend_backward(first, heads, bad, q, kv_other, kv, kv_partner, grad, mixed, lse, after):
    tokens = q.shape[3]
    return pl.pallas_call(
        backward_kernel,
        grid=(heads,),
        in_specs=[pl.BlockSpec(memory_space=pltpu.SMEM), heads_spec(first, 1, tokens)]
        + [heads_spec(first, 2, tokens)] * 3
        + [heads_spec(first, 1, tokens)] * 2
        + [pl.BlockSpec((1, 1, ROWS * tokens), lambda i: (first + i, 0, 0))]
        + [pl.BlockSpec(memory_space=pl.ANY)] * len(after),
        out_specs=[heads_spec(0, 1, tokens)] + [heads_spec(0, 2, tokens)] * 3,
        out_shape=[bf16(ROWS, heads, 1, tokens, HEAD_DIM)]
        + [bf16(ROWS, heads, 2, tokens, HEAD_DIM)] * 3,
        scratch_shapes=[
            pltpu.VMEM((HEAD_DIM, ROWS * tokens), jnp.float32),
            pltpu.VMEM((1, ROWS * tokens), jnp.float32),
        ],
        cost_estimate=cost(100),
        compiler_params=params(),
    )(bad, q, kv_other, kv, kv_partner, grad, mixed, lse, *after)


def add_terms(refs, row, head, tensor):
    terms = [ref[row, head, tensor].astype(jnp.float32) for ref in refs]
    return functools.reduce(jnp.add, terms).astype(jnp.bfloat16)


def early_kernel(dq_ref, *refs):
    terms, late_ref, out_ref = refs[:3], refs[3], refs[-1]
    for r in range(ROWS):
        out_ref[r, 0] = dq_ref[r, 0, 0]
        for t in range(2):
            out_ref[r, 1 + t] = add_terms(terms, r, 0, t)
        for h in range(late_ref.shape[1]):
            out_ref[r, 3 + h] = late_ref[r, h, 0]


def late_kernel(*refs):
    terms, out_ref = refs[:3], refs[-1]
    for r in range(ROWS):
        for h in range(terms[0].shape[1]):
            for t in range(2):
                out_ref[r, 2 * h + t] = add_terms(terms, r, h, t)


def totals(kernel, slots, arrays, after=(), told=0.1):
    tokens = arrays[0].shape[3]
    vmem = pl.BlockSpec(memory_space=pltpu.VMEM)
    return pl.pallas_call(
        kernel,
        in_specs=[vmem] * len(arrays) + [pl.BlockSpec(memory_space=pl.ANY)] * len(after),
        out_specs=vmem,
        out_shape=bf16(ROWS, slots, tokens, HEAD_DIM),
        cost_estimate=cost(told),
        compiler_params=params(),
    )(*arrays, *after)


def lane_sums(products):
    rows = products[0].shape[0]
    product = jnp.concatenate(products, axis=0)
    high = product.astype(jnp.bfloat16)
    low = (product - high.astype(jnp.float32)).astype(jnp.bfloat16)
    ones = jnp.ones((2 * HEAD_DIM, HEAD_DIM), jnp.bfloat16)
    sums = dot(jnp.concatenate([high, low], axis=1), ones, NN)
    return [sums[i * rows : (i + 1) * rows] for i in range(len(products))]


def temporal_weights(probes, anchors):
    scores = lane_sums([p * a for p in probes for a in anchors])
    weights = []
    for f in range(PARTS):
        row = [s * SCALE for s in scores[f * PARTS : (f + 1) * PARTS]]
        top = functools.reduce(jnp.maximum, row)
        shifted = [jnp.exp(s - top) for s in row]
        inverse = 1.0 / functools.reduce(jnp.add, shifted)
        weights.append([s * inverse for s in shifted])
    return weights


def rounded(x):
    return x.astype(jnp.bfloat16).astype(jnp.float32)


def temporal_forward_kernel(*refs):
    ins, outs = refs[:PARTS], refs[-PARTS:]
    parts = [[ref[0, t].astype(jnp.float32) for ref in ins] for t in range(3)]
    weights = temporal_weights(parts[0], parts[1])
    for g in range(PARTS):
        terms = [rounded(weights[f][g]) * parts[2][f] for f in range(PARTS)]
        outs[g][0, 0] = functools.reduce(jnp.add, terms).astype(jnp.bfloat16)


def temporal_backward_kernel(*refs):
    ins, mixed_refs, outs = refs[:PARTS], refs[PARTS : 2 * PARTS], refs[-PARTS:]
    parts = [[ref[0, t].astype(jnp.float32) for ref in ins] for t in range(3)]
    mixed = [ref[0, 0].astype(jnp.float32) for ref in mixed_refs]
    weights = temporal_weights(parts[0], parts[1])
    sums = lane_sums([u * m for u in parts[2] for m in mixed])
    anchor_grads = [None] * PARTS
    for f in range(PARTS):
        grads = sums[f * PARTS : (f + 1) * PARTS]
        row = functools.reduce(jnp.add, [w * c for w, c in zip(weights[f], grads)])
        scores = [rounded(w * (c - row)) for w, c in zip(weights[f], grads)]
        probe = functools.reduce(jnp.add, [s * parts[1][g] for g, s in enumerate(scores)])
        outs[f][0, 0] = (probe * SCALE).astype(jnp.bfloat16)
        for g in range(PARTS):
            term = scores[g] * parts[0][f]
            anchor_grads[g] = term if f == 0 else anchor_grads[g] + term
    for g in range(PARTS):
        outs[g][0, 1] = (anchor_grads[g] * SCALE).astype(jnp.bfloat16)


def temporal_call(kernel, arrays, count_out, told, after=()):
    group, _, tokens, _ = arrays[0].shape
    rows = 256

    def spec(count):
        return pl.BlockSpec((1, count, rows, HEAD_DIM), lambda h, i: (h, 0, i, 0))

    return pl.pallas_call(
        kernel,
        grid=(group, tokens // rows),
        in_specs=[spec(a.shape[1]) for a in arrays]
        + [pl.BlockSpec(memory_space=pl.ANY)] * len(after),
        out_specs=[spec(count_out)] * PARTS,
        out_shape=[bf16(group, count_out, tokens, HEAD_DIM)] * PARTS,
        cost_estimate=cost(told),
        compiler_params=params(),
    )(*arrays, *after)


def swap(x, axis):
    return lax.all_to_all(x, axis, split_axis=0, concat_axis=0, tiled=True)


def trade_partner(x):
    return lax.ppermute(x, "wa", [(i, i ^ 1) for i in range(lax.axis_size("wa"))])


def trade_other(x):
    firsts = range(1, lax.axis_size("wa") - 1, 2)
    pairs = [(i, i + 1) for i in firsts] + [(i + 1, i) for i in firsts]
    return lax.ppermute(x, "wa", pairs)


def shards(queries, tile_keys, values, probes, anchors, upstream):
    shape = queries.shape
    tokens = shape[2] * shape[3]

    def flat(x):
        return x.reshape(tokens, shape[-1])

    place = lax.axis_index("wa")
    no_other = (place == 0) | (place == lax.axis_size("wa") - 1)
    bad = no_other.astype(jnp.float32).reshape(1) * BIG

    kv_sent = pack([flat(tile_keys), flat(values)])
    kv = swap(kv_sent, "ha")
    kv_other = trade_other(kv)
    kv_partner = trade_partner(kv)
    pau_sent = pack_partners([flat(probes), flat(anchors), flat(upstream)], [kv_sent])
    pau = trade(pau_sent)
    q_sent = pack([flat(queries)], pau_sent[:1])
    q = swap(q_sent, "ha")
    grad_parts = trade(temporal_call(temporal_forward_kernel, pau, 1, 10, [kv, q_sent]))
    grad_sent = join_partners(grad_parts)
    grad = swap(grad_sent, "ha")
    mixed, lse = attend_forward(bad, q, kv_other, kv, kv_partner, grad_sent)
    mixed_sent = split_partners(swap(mixed, "ha"))
    mixed_parts = trade(mixed_sent)
    def backward(first, heads, after):
        dq, to_other, own, to_partner = attend_backward(
            first, heads, bad, q, kv_other, kv, kv_partner, grad, mixed, lse, after
        )
        return dq, own, trade_other(to_other), trade_partner(to_partner)

    one = backward(0, 1, [])
    two = backward(1, GROUP - 1, [mixed_sent[0], one[0]])
    early = totals(early_kernel, GROUP + 2, (*one, two[0]), told=0.1)
    times_sent = temporal_call(
        temporal_backward_kernel, pau + mixed_parts, 2, 5, [early]
    )
    early = swap(early, "ha")
    late = swap(totals(late_kernel, 2 * (GROUP - 1), two[1:], [early]), "ha")
    probe_grad, anchor_grad = unpack_partners(trade(times_sent), [])
    query_grad, key_grad, value_grad = unpack_heads(early, late)
    outs = (query_grad, key_grad, value_grad, probe_grad, anchor_grad)
    return tuple(x.reshape(shape) for x in outs)


def solution(mesh):
    spec = P(None, "tm", "ha", "wa", None)
    return jax.shard_map(
        shards,
        mesh=mesh,
        in_specs=(spec,) * 6,
        out_specs=(spec,) * 5,
        check_vma=False,
    )
```

```python
import functools

import jax
import jax.numpy as jnp
from jax import lax
from jax.experimental import pallas as pl
from jax.experimental.pallas import tpu as pltpu
from jax.sharding import PartitionSpec as P

HEADS = 12
HEAD_DIM = 128
PARTS = 4
GROUP = HEADS // PARTS
ROWS = 4
BIG = 1e30
SCALE = HEAD_DIM ** (-0.5)
LOG2E = 1.4426950408889634
BASE2 = SCALE * LOG2E

NT = (((1,), (1,)), ((), ()))
NN = (((1,), (0,)), ((), ()))
TN = (((0,), (0,)), ((), ()))


def dot(a, b, dims):
    return lax.dot_general(a, b, dims, preferred_element_type=jnp.float32)


def params():
    return pltpu.CompilerParams(vmem_limit_bytes=64 * 1024 * 1024)


def cost(microseconds):
    return pl.CostEstimate(
        flops=int(microseconds * 1e9), bytes_accessed=1024, transcendentals=0
    )


def move(inputs, out_shapes, plan, axis=None, after=(), told=0.1):
    first = len(inputs) + len(after)

    def kernel(*refs):
        ins = refs[: len(inputs)]
        outs = refs[first:]
        me = 0 if axis is None else lax.axis_index(axis)
        for i, at, o, to in plan(me):
            outs[o][to] = ins[i][at]

    return pl.pallas_call(
        kernel,
        in_specs=[pl.BlockSpec(memory_space=pltpu.VMEM)] * len(inputs)
        + [pl.BlockSpec(memory_space=pl.ANY)] * len(after),
        out_specs=[pl.BlockSpec(memory_space=pltpu.VMEM)] * len(out_shapes),
        out_shape=out_shapes,
        cost_estimate=cost(told),
        compiler_params=params(),
    )(*inputs, *after)


def columns(group, head):
    start = (group * GROUP + head) * HEAD_DIM
    if not isinstance(start, int):
        start = pl.multiple_of(start, HEAD_DIM)
    return (slice(None), pl.ds(start, HEAD_DIM))


def bf16(*shape):
    return jax.ShapeDtypeStruct(shape, jnp.bfloat16)


def pack(arrays, after=(), told=0.1):
    tokens = arrays[0].shape[0]
    cells = [(a, d, h) for d in range(PARTS) for h in range(GROUP) for a in range(len(arrays))]
    return move(
        arrays,
        [bf16(PARTS, GROUP, len(arrays), tokens, HEAD_DIM)],
        lambda me: [(a, columns(d, h), 0, (d, h, a)) for a, d, h in cells],
        after=after,
        told=told,
    )[0]


def pack_partners(arrays, after=()):
    tokens = arrays[0].shape[0]
    cells = [(a, s, h) for s in range(PARTS) for h in range(GROUP) for a in range(len(arrays))]
    return move(
        arrays,
        [bf16(GROUP, len(arrays), tokens, HEAD_DIM)] * PARTS,
        lambda me: [(a, columns(me ^ s, h), s, (h, a)) for a, s, h in cells],
        "tm",
        after,
    )


def unpack_partners(chunks, after):
    _, count, tokens, _ = chunks[0].shape
    cells = [(a, s, h) for s in range(PARTS) for h in range(GROUP) for a in range(count)]
    return move(
        chunks,
        [bf16(tokens, HEADS * HEAD_DIM)] * count,
        lambda me: [(s, (h, a), a, columns(me ^ s, h)) for a, s, h in cells],
        "tm",
        after,
        told=100,
    )


def join_partners(chunks):
    return move(
        chunks,
        [bf16(PARTS, *chunks[0].shape)],
        lambda me: [(s, (slice(None),), 0, (me ^ s,)) for s in range(PARTS)],
        "tm",
    )[0]


def split_partners(block):
    return move(
        [block],
        [bf16(*block.shape[1:])] * PARTS,
        lambda me: [(0, (me ^ s,), s, (slice(None),)) for s in range(PARTS)],
        "tm",
    )


def unpack_slots(blocks, places, told=0.1):
    tokens = blocks[0].shape[2]
    cells = [(a, d, h) for h in range(GROUP) for d in range(PARTS) for a in range(len(places))]
    return move(
        blocks,
        [bf16(tokens, HEADS * HEAD_DIM)] * len(places),
        lambda me: [
            (places[a][h][0], (d, places[a][h][1]), a, columns(d, h)) for a, d, h in cells
        ],
        told=told,
    )


def trade(chunks):
    out = [chunks[0]]
    for s in range(1, PARTS):
        out.append(lax.ppermute(chunks[s], "tm", [(i, i ^ s) for i in range(PARTS)]))
    return out


def near_rows(row):
    return max(row - 1, 0), min(row + 2, ROWS)


def tiles(ref, rows, tensor):
    low, high = rows
    block = ref[low:high, 0, tensor]
    return block.reshape((high - low) * block.shape[1], HEAD_DIM)


def forward_kernel(bad_ref, q_ref, other_ref, own_ref, partner_ref, _, o_ref, lse_ref, vt_ref):
    bad = bad_ref[0]
    sides = (other_ref, own_ref, partner_ref)
    tokens = q_ref.shape[3]
    for side in range(3):
        vt_ref[side] = tiles(sides[side], (0, ROWS), 1).T
    for b in range(ROWS):
        query = q_ref[b, 0, 0]
        rows = near_rows(b)
        span = slice(rows[0] * tokens, rows[1] * tokens)
        scores = [dot(tiles(ref, rows, 0), query, NT) for ref in sides]
        tops = [jnp.max(s, axis=0, keepdims=True) for s in scores]
        top = functools.reduce(jnp.maximum, [tops[0] - bad] + tops[1:]) * BASE2
        total = None
        mixed = None
        for side, s in enumerate(scores):
            p = jnp.exp2(s * BASE2 - (top + bad if side == 0 else top))
            one = jnp.sum(p, axis=0, keepdims=True)
            total = one if total is None else total + one
            term = dot(vt_ref[side, :, span], p.astype(jnp.bfloat16), NN)
            mixed = term if mixed is None else mixed + term
        mixed = mixed * (1.0 / total)
        o_ref[b, 0, 0] = mixed.T.astype(jnp.bfloat16)
        lse_ref[0, :, b * tokens : (b + 1) * tokens] = top + jnp.log2(total)


def column_spec(count, tokens):
    return pl.BlockSpec((ROWS, 1, count, tokens, HEAD_DIM), lambda h: (0, h, 0, 0, 0))


def attend_forward(bad, q, kv_other, kv, kv_partner, after):
    tokens = q.shape[3]
    group = q.shape[1]
    return pl.pallas_call(
        forward_kernel,
        grid=(group,),
        in_specs=[pl.BlockSpec(memory_space=pltpu.SMEM), column_spec(1, tokens)]
        + [column_spec(2, tokens)] * 3
        + [pl.BlockSpec(memory_space=pl.ANY)],
        out_specs=[
            column_spec(1, tokens),
            pl.BlockSpec((1, 1, ROWS * tokens), lambda h: (h, 0, 0)),
        ],
        out_shape=[
            jax.ShapeDtypeStruct(q.shape, jnp.bfloat16),
            jax.ShapeDtypeStruct((group, 1, ROWS * tokens), jnp.float32),
        ],
        scratch_shapes=[pltpu.VMEM((3, HEAD_DIM, ROWS * tokens), jnp.bfloat16)],
        cost_estimate=cost(100),
        compiler_params=params(),
    )(bad, q, kv_other, kv, kv_partner, after)


def backward_kernel(
    bad_ref, q_ref, other_ref, own_ref, partner_ref, do_ref, o_ref, lse_ref, *rest
):
    dq_ref, d_other_ref, d_own_ref, d_partner_ref, dqt_ref, row_ref = rest[-6:]
    bad = bad_ref[0]
    sides = (other_ref, own_ref, partner_ref)
    outs = (d_other_ref, d_own_ref, d_partner_ref)
    tokens = q_ref.shape[3]
    for b in range(ROWS):
        product = do_ref[b, 0, 0].astype(jnp.float32) * o_ref[b, 0, 0].astype(jnp.float32)
        row_ref[:, b * tokens : (b + 1) * tokens] = jnp.sum(product.T, axis=0, keepdims=True)
    dqt_ref[...] = jnp.zeros_like(dqt_ref)
    for side in range(3):
        for u in range(ROWS):
            rows = near_rows(u)
            span = slice(rows[0] * tokens, rows[1] * tokens)
            key = sides[side][u, 0, 0]
            query = tiles(q_ref, rows, 0)
            grad = tiles(do_ref, rows, 0)
            lse = lse_ref[0, :, span]
            if side == 0:
                lse = lse + bad
            p = jnp.exp2(dot(key, query, NT) * BASE2 - lse)
            e = dot(sides[side][u, 0, 1], grad, NT)
            g = (p * (e - row_ref[:, span])).astype(jnp.bfloat16)
            dk = dot(g, query, NN) * SCALE
            dv = dot(p.astype(jnp.bfloat16), grad, NN)
            dqt_ref[:, span] += dot(key, g, TN)
            outs[side][u, 0, 0] = dk.astype(outs[side].dtype)
            outs[side][u, 0, 1] = dv.astype(outs[side].dtype)
    for b in range(ROWS):
        dq = dqt_ref[:, b * tokens : (b + 1) * tokens] * SCALE
        dq_ref[b, 0, 0] = dq.T.astype(jnp.bfloat16)


def heads_spec(first, count, tokens):
    return pl.BlockSpec((ROWS, 1, count, tokens, HEAD_DIM), lambda i: (0, first + i, 0, 0, 0))


def attend_backward(first, heads, bad, q, kv_other, kv, kv_partner, grad, mixed, lse, after):
    tokens = q.shape[3]
    return pl.pallas_call(
        backward_kernel,
        grid=(heads,),
        in_specs=[pl.BlockSpec(memory_space=pltpu.SMEM), heads_spec(first, 1, tokens)]
        + [heads_spec(first, 2, tokens)] * 3
        + [heads_spec(first, 1, tokens)] * 2
        + [pl.BlockSpec((1, 1, ROWS * tokens), lambda i: (first + i, 0, 0))]
        + [pl.BlockSpec(memory_space=pl.ANY)] * len(after),
        out_specs=[heads_spec(0, 1, tokens)] + [heads_spec(0, 2, tokens)] * 3,
        out_shape=[bf16(ROWS, heads, 1, tokens, HEAD_DIM)]
        + [bf16(ROWS, heads, 2, tokens, HEAD_DIM)] * 3,
        scratch_shapes=[
            pltpu.VMEM((HEAD_DIM, ROWS * tokens), jnp.float32),
            pltpu.VMEM((1, ROWS * tokens), jnp.float32),
        ],
        cost_estimate=cost(100),
        compiler_params=params(),
    )(bad, q, kv_other, kv, kv_partner, grad, mixed, lse, *after)


def add_terms(refs, row, head, tensor):
    terms = [ref[row, head, tensor].astype(jnp.float32) for ref in refs]
    return functools.reduce(jnp.add, terms).astype(jnp.bfloat16)


def early_kernel(dq_ref, *refs):
    terms, late_ref, out_ref = refs[:3], refs[3], refs[-1]
    for r in range(ROWS):
        out_ref[r, 0] = dq_ref[r, 0, 0]
        for t in range(2):
            out_ref[r, 1 + t] = add_terms(terms, r, 0, t)
        for h in range(late_ref.shape[1]):
            out_ref[r, 3 + h] = late_ref[r, h, 0]


def late_kernel(*refs):
    terms, out_ref = refs[:3], refs[-1]
    for r in range(ROWS):
        for h in range(terms[0].shape[1]):
            for t in range(2):
                out_ref[r, 2 * h + t] = add_terms(terms, r, h, t)


def totals(kernel, slots, arrays, after=(), told=0.1):
    tokens = arrays[0].shape[3]
    vmem = pl.BlockSpec(memory_space=pltpu.VMEM)
    return pl.pallas_call(
        kernel,
        in_specs=[vmem] * len(arrays) + [pl.BlockSpec(memory_space=pl.ANY)] * len(after),
        out_specs=vmem,
        out_shape=bf16(ROWS, slots, tokens, HEAD_DIM),
        cost_estimate=cost(told),
        compiler_params=params(),
    )(*arrays, *after)


def lane_sums(products):
    rows = products[0].shape[0]
    product = jnp.concatenate(products, axis=0)
    high = product.astype(jnp.bfloat16)
    low = (product - high.astype(jnp.float32)).astype(jnp.bfloat16)
    ones = jnp.ones((2 * HEAD_DIM, HEAD_DIM), jnp.bfloat16)
    sums = dot(jnp.concatenate([high, low], axis=1), ones, NN)
    return [sums[i * rows : (i + 1) * rows] for i in range(len(products))]


def temporal_weights(probes, anchors):
    scores = lane_sums([p * a for p in probes for a in anchors])
    weights = []
    for f in range(PARTS):
        row = [s * SCALE for s in scores[f * PARTS : (f + 1) * PARTS]]
        top = functools.reduce(jnp.maximum, row)
        shifted = [jnp.exp(s - top) for s in row]
        inverse = 1.0 / functools.reduce(jnp.add, shifted)
        weights.append([s * inverse for s in shifted])
    return weights


def rounded(x):
    return x.astype(jnp.bfloat16).astype(jnp.float32)


def temporal_forward_kernel(*refs):
    ins, outs = refs[:PARTS], refs[-PARTS:]
    parts = [[ref[0, t].astype(jnp.float32) for ref in ins] for t in range(3)]
    weights = temporal_weights(parts[0], parts[1])
    for g in range(PARTS):
        terms = [rounded(weights[f][g]) * parts[2][f] for f in range(PARTS)]
        outs[g][0, 0] = functools.reduce(jnp.add, terms).astype(jnp.bfloat16)


def temporal_backward_kernel(*refs):
    ins, mixed_refs, outs = refs[:PARTS], refs[PARTS : 2 * PARTS], refs[-PARTS:]
    parts = [[ref[0, t].astype(jnp.float32) for ref in ins] for t in range(3)]
    mixed = [ref[0, 0].astype(jnp.float32) for ref in mixed_refs]
    weights = temporal_weights(parts[0], parts[1])
    sums = lane_sums([u * m for u in parts[2] for m in mixed])
    anchor_grads = [None] * PARTS
    for f in range(PARTS):
        grads = sums[f * PARTS : (f + 1) * PARTS]
        row = functools.reduce(jnp.add, [w * c for w, c in zip(weights[f], grads)])
        scores = [rounded(w * (c - row)) for w, c in zip(weights[f], grads)]
        probe = functools.reduce(jnp.add, [s * parts[1][g] for g, s in enumerate(scores)])
        outs[f][0, 0] = (probe * SCALE).astype(jnp.bfloat16)
        for g in range(PARTS):
            term = scores[g] * parts[0][f]
            anchor_grads[g] = term if f == 0 else anchor_grads[g] + term
    for g in range(PARTS):
        outs[g][0, 1] = (anchor_grads[g] * SCALE).astype(jnp.bfloat16)


def temporal_call(kernel, arrays, count_out, told, after=()):
    group, _, tokens, _ = arrays[0].shape
    rows = 256

    def spec(count):
        return pl.BlockSpec((1, count, rows, HEAD_DIM), lambda h, i: (h, 0, i, 0))

    return pl.pallas_call(
        kernel,
        grid=(group, tokens // rows),
        in_specs=[spec(a.shape[1]) for a in arrays]
        + [pl.BlockSpec(memory_space=pl.ANY)] * len(after),
        out_specs=[spec(count_out)] * PARTS,
        out_shape=[bf16(group, count_out, tokens, HEAD_DIM)] * PARTS,
        cost_estimate=cost(told),
        compiler_params=params(),
    )(*arrays, *after)


def swap(x, axis):
    return lax.all_to_all(x, axis, split_axis=0, concat_axis=0, tiled=True)


def trade_partner(x):
    return lax.ppermute(x, "wa", [(i, i ^ 1) for i in range(lax.axis_size("wa"))])


def trade_other(x):
    firsts = range(1, lax.axis_size("wa") - 1, 2)
    pairs = [(i, i + 1) for i in firsts] + [(i + 1, i) for i in firsts]
    return lax.ppermute(x, "wa", pairs)


def shards(queries, tile_keys, values, probes, anchors, upstream):
    shape = queries.shape
    tokens = shape[2] * shape[3]

    def flat(x):
        return x.reshape(tokens, shape[-1])

    place = lax.axis_index("wa")
    no_other = (place == 0) | (place == lax.axis_size("wa") - 1)
    bad = no_other.astype(jnp.float32).reshape(1) * BIG

    kv_sent = pack([flat(tile_keys), flat(values)])
    kv = swap(kv_sent, "ha")
    kv_other = trade_other(kv)
    kv_partner = trade_partner(kv)
    pau_sent = pack_partners([flat(probes), flat(anchors), flat(upstream)], [kv_sent])
    pau = trade(pau_sent)
    q_sent = pack([flat(queries)], pau_sent[:1])
    q = swap(q_sent, "ha")
    grad_parts = trade(temporal_call(temporal_forward_kernel, pau, 1, 10, [kv, q_sent]))
    grad_sent = join_partners(grad_parts)
    grad = swap(grad_sent, "ha")
    mixed, lse = attend_forward(bad, q, kv_other, kv, kv_partner, grad_sent)
    mixed_sent = split_partners(swap(mixed, "ha"))
    mixed_parts = trade(mixed_sent)
    def backward(first, heads, after):
        dq, to_other, own, to_partner = attend_backward(
            first, heads, bad, q, kv_other, kv, kv_partner, grad, mixed, lse, after
        )
        return dq, own, trade_other(to_other), trade_partner(to_partner)

    one = backward(0, 1, [])
    two = backward(1, GROUP - 1, [mixed_sent[0], one[0]])
    early = totals(early_kernel, GROUP + 2, (*one, two[0]), told=0.1)
    times_sent = temporal_call(
        temporal_backward_kernel, pau + mixed_parts, 2, 5, [early]
    )
    early = swap(early, "ha")
    late = swap(totals(late_kernel, 2 * (GROUP - 1), two[1:], [early]), "ha")
    late_heads = range(GROUP - 1)
    (query_grad,) = unpack_slots([early], [[(0, 0)] + [(0, 3 + h) for h in late_heads]], 100)
    probe_grad, anchor_grad = unpack_partners(trade(times_sent), [query_grad])
    key_grad, value_grad = unpack_slots(
        [early, late],
        [[(0, 1 + t)] + [(1, 2 * h + t) for h in late_heads] for t in range(2)],
    )
    outs = (query_grad, key_grad, value_grad, probe_grad, anchor_grad)
    return tuple(x.reshape(shape) for x in outs)


def solution(mesh):
    spec = P(None, "tm", "ha", "wa", None)
    return jax.shard_map(
        shards,
        mesh=mesh,
        in_specs=(spec,) * 6,
        out_specs=(spec,) * 5,
        check_vma=False,
    )
```
